256 devices in a mesh: ulysses: 8 (over x, core), blk: 32 (over y, z).
Axes of the slice: x: 4, y: 4, z: 8, core: 2. Of those that a mesh axis runs over, the one named last changes fastest.
Arguments:
- query: bfloat16 [49152, 8, 128], P(('blk', 'ulysses')), may hold values from -6 to 6
- key: bfloat16 [49152, 128], P(('blk', 'ulysses')), may hold values from -6 to 6
- value: bfloat16 [49152, 128], P(('blk', 'ulysses')), may hold values from -6 to 6
- output: bfloat16 [49152, 8, 128], P(('blk', 'ulysses')), may hold values from -0.59765625 to 0.59765625
- grad_out: bfloat16 [49152, 8, 128], P(('blk', 'ulysses')), may hold values from -6 to 6
- lse: float32 [8, 49152], P(None, ('blk', 'ulysses')), may hold values from 4 to 7
- doc_lengths: int32 [32], replicated, may hold values from 1 to 3072, 49152 in all
Outputs:
- grad_query: bfloat16 [49152, 8, 128], P(('blk', 'ulysses'))
- grad_key: bfloat16 [49152, 128], P(('blk', 'ulysses'))
- grad_value: bfloat16 [49152, 128], P(('blk', 'ulysses'))
The draws below stay inside these ranges and needn't reach their ends.
Inputs may be any that keep to these rules, and one draw needn't show every extreme that they name: `doc_lengths`: the documents are laid end to end from position 0 and fill all 49152 positions; the longest has exactly 3072 tokens.
All inputs are finite; a program needn't handle non-finite values.
Results may differ from the reference program's by a relative error of at most 0.024.
Values may be sent and summed in bfloat16 or wider, within the bound.
A program may use at most 64 MiB of HBM per device.

```python
import math
import jax
import jax.numpy as jnp
import numpy as np
from jax import lax

GROUP = 8
HEAD_DIM = 128
SEQ = 49152
DOC_MAX = 3072
NDOCS = 32


def steps_of(key, shape, cuts, low, top_value):
    def one(dim, parts):
        steps = jax.random.uniform(jax.random.fold_in(jax.random.fold_in(key, 6), dim), (parts,), jnp.float32, low / len(cuts), top_value / len(cuts))
        return jnp.repeat(jnp.exp(steps), shape[dim] // parts).reshape((-1,) + (1,) * (len(shape) - dim - 1))

    loudness = one(*cuts[0])
    for cut in cuts[1:]:
        loudness = loudness * one(*cut)
    return loudness


def profile(count, total, reach, slope):
    portions = [(1 << 20) // math.isqrt(grade ** slope) + 1 for grade in range(2, count + 1)]
    rest, given = total - reach - (count - 1), [1] * (count - 1)
    while rest > 0:
        candidates = [i for i in range(count - 1) if given[i] < reach]
        pool, remaining = sum([portions[i] for i in candidates]), rest
        for i in candidates:
            extra = min(reach - given[i], max(1, remaining * portions[i] // pool), rest)
            given[i] = given[i] + extra
            rest = rest - extra
    return np.array([reach] + given)


def ragged(key, number_of, total, limit, lean):
    if number_of == 2:
        one = jax.random.randint(key, (), max(1, total - limit), min(limit, total - 1) + 1)
        return jnp.stack([one, total - one])
    lengths = jnp.asarray(profile(number_of, total, limit, lean), jnp.int32)
    couples = (number_of - 1) // 2
    giver, taker = lengths[1:1 + 2 * couples:2], lengths[2:2 + 2 * couples:2]
    room = jnp.minimum(giver - 1, limit - taker)
    shifted = jax.random.randint(jax.random.fold_in(key, 1), (couples,), 0, 1 << 20) % (room + 1)
    lengths = lengths.at[1:1 + 2 * couples:2].set(giver - shifted).at[2:2 + 2 * couples:2].set(taker + shifted)
    return lengths[jax.random.permutation(jax.random.fold_in(key, 2), number_of)]


def normal_values(rng, shape, width, reach, pieces=(), kind=jnp.bfloat16):
    level = steps_of(rng, shape, pieces, -0.22, 0.18) if pieces else 1.0
    result = jax.random.normal(rng, shape, jnp.float32) * width * level
    return jnp.minimum(jnp.maximum(result, -reach), reach).astype(kind)


def setup_inputs(seed: int = 0) -> dict:
    key_list = jax.random.split(jax.random.key(seed), 8)
    query = normal_values(key_list[0], (SEQ, GROUP, HEAD_DIM), 1.0, 6.0, ((0, 256),))
    key = normal_values(key_list[1], (SEQ, HEAD_DIM), 1.0, 6.0, ((0, 256),))
    value = normal_values(key_list[2], (SEQ, HEAD_DIM), 1.0, 6.0, ((0, 256),))
    output = normal_values(key_list[3], (SEQ, GROUP, HEAD_DIM), 0.1, 0.59765625, ((0, 256),))
    grad_out = normal_values(key_list[4], (SEQ, GROUP, HEAD_DIM), 1.0, 6.0, ((0, 256),))
    lse = jnp.clip(4.0 + 3.0 * jax.random.uniform(key_list[5], (GROUP, SEQ), jnp.float32) ** steps_of(key_list[5], (GROUP, SEQ), ((1, 256),), -0.2, 0.2), 4.0, 7.0)
    doc_lengths = ragged(key_list[6], NDOCS, SEQ, DOC_MAX, 2).astype(jnp.int32)
    return {"query": query, "key": key, "value": value, "output": output, "grad_out": grad_out, "lse": lse, "doc_lengths": doc_lengths}


def doc_ids(positions, ends):
    return jnp.sum((ends[None, :] <= positions[:, None]).astype(jnp.int32), axis=1)


def reference(query, key, value, output, grad_out, lse, doc_lengths):
    scale = HEAD_DIM ** -0.5
    ends = jnp.cumsum(doc_lengths).astype(jnp.int32)
    delta = jnp.einsum("thd,thd->th", grad_out.astype(jnp.float32), output.astype(jnp.float32))
    qblock = math.gcd(SEQ, 512)
    nblocks = SEQ // qblock
    margin = DOC_MAX
    window = margin + qblock
    key_pad = jnp.concatenate([jnp.zeros((margin, HEAD_DIM), jnp.bfloat16), key], axis=0)
    val_pad = jnp.concatenate([jnp.zeros((margin, HEAD_DIM), jnp.bfloat16), value], axis=0)
    offsets = jnp.arange(qblock, dtype=jnp.int32)
    koffsets = jnp.arange(window, dtype=jnp.int32)

    def one(carry, index):
        dk_pad, dv_pad = carry
        start = (index * qblock).astype(jnp.int32)
        qpart = lax.dynamic_slice_in_dim(query, start, qblock, 0).astype(jnp.float32)
        dpart = lax.dynamic_slice_in_dim(grad_out, start, qblock, 0).astype(jnp.float32)
        lpart = lax.dynamic_slice_in_dim(lse, start, qblock, 1)
        epart = lax.dynamic_slice_in_dim(delta, start, qblock, 0)
        kpart = lax.dynamic_slice_in_dim(key_pad, start, window, 0).astype(jnp.float32)
        vpart = lax.dynamic_slice_in_dim(val_pad, start, window, 0).astype(jnp.float32)
        qpos = start + offsets
        kpos = start - margin + koffsets
        allowed = (doc_ids(qpos, ends)[:, None] == doc_ids(kpos, ends)[None, :]) & (kpos[None, :] <= qpos[:, None]) & (kpos[None, :] >= 0)
        scores = jnp.einsum("qhd,kd->hqk", qpart, kpart) * scale
        probs = jnp.where(allowed[None], jnp.exp(scores - lpart[:, :, None]), 0.0)
        rounded = probs.astype(jnp.bfloat16).astype(jnp.float32)
        dv_term = jnp.einsum("hqk,qhd->kd", rounded, dpart)
        dprobs = jnp.einsum("qhd,kd->hqk", dpart, vpart)
        dscores = (probs * (dprobs - epart.T[:, :, None])).astype(jnp.bfloat16).astype(jnp.float32)
        dq_part = jnp.einsum("hqk,kd->qhd", dscores, kpart) * scale
        dk_term = jnp.einsum("hqk,qhd->kd", dscores, qpart)
        dk_pad = lax.dynamic_update_slice_in_dim(dk_pad, lax.dynamic_slice_in_dim(dk_pad, start, window, 0) + dk_term, start, 0)
        dv_pad = lax.dynamic_update_slice_in_dim(dv_pad, lax.dynamic_slice_in_dim(dv_pad, start, window, 0) + dv_term, start, 0)
        return (dk_pad, dv_pad), dq_part.astype(jnp.bfloat16)

    zeros = jnp.zeros((margin + SEQ, HEAD_DIM), jnp.float32)
    (dk_pad, dv_pad), dq_blocks = lax.scan(one, (zeros, zeros), jnp.arange(nblocks, dtype=jnp.int32))
    grad_query = dq_blocks.reshape(SEQ, GROUP, HEAD_DIM)
    grad_key = (dk_pad[margin:] * scale).astype(jnp.bfloat16)
    grad_value = dv_pad[margin:].astype(jnp.bfloat16)
    return (grad_query, grad_key, grad_value)
```

```python
import math

import jax
import jax.numpy as jnp
from jax import lax
from jax.experimental import pallas as pl
from jax.experimental.pallas import tpu as pltpu
from jax.sharding import PartitionSpec as P

f32 = jnp.float32
bf16 = jnp.bfloat16
MESH = pl.DeviceIdType.MESH

HEADS = 8
WIDTH = 128
TOKENS = 192
ROWS = TOKENS * HEADS
GROUPS = 8
BLOCK = TOKENS * GROUPS
BLOCKS = 32
CHIPS = 4
NDOCS = 32
KEYS = 4 * TOKENS
HALF = ROWS // 2
SCALE = WIDTH ** -0.5
RATE = SCALE * math.log2(math.e)
FAR = float(2 ** 17)
LSE_LANE = NDOCS
FEATURES = NDOCS + 3 * HEADS

Z_IN = 0
X_IN = 2
C_IN = 8
C_OUT = 16
X_OUT = 24
Z_OUT = 30
MESSAGES = 32


def dot(a, b, ca, cb):
    return lax.dot_general(a, b, (((ca,), (cb,)), ((), ())), preferred_element_type=f32)


def three_parts(value):
    high = value.astype(bf16).astype(f32)
    middle = (value - high).astype(bf16).astype(f32)
    return high, middle, value - high - middle


def slot_of(dx, old, other):
    return dx * 4 + old * 2 + other


def kernel(
    len_ref, q_ref, k_ref, v_ref, o_ref, do_ref, lse_ref,
    dq_ref, dk_ref, dv_ref,
    own, slots, qx, dox, q_t, do_t, kx, vx, dq_acc, dk_acc, dv_acc, lse_pad,
    diag, part, c_in, x_out, x_in, z_out, z_in, send_sem, recv_sem,
):
    block = lax.axis_index("blk")
    index = lax.axis_index("ulysses")
    x = index // 2
    core = lax.rem(index, 2)

    def column(d):
        return {"blk": block, "ulysses": lax.rem(x + d, CHIPS) * 2 + core}

    def behind(steps):
        return {"blk": lax.rem(block + steps + BLOCKS, BLOCKS), "ulysses": index}

    partner = {"blk": block, "ulysses": x * 2 + 1 - core}

    barrier = pltpu.get_barrier_semaphore()
    others = [partner] + [column(d) for d in (1, 2, 3)] + [behind(s) for s in (1, 2, -1, -2)]
    for device in others:
        pl.semaphore_signal(barrier, inc=1, device_id=device, device_id_type=MESH)

    def message(number, source, target, device):
        return pltpu.make_async_remote_copy(
            src_ref=source,
            dst_ref=target,
            send_sem=send_sem.at[number],
            recv_sem=recv_sem.at[number],
            device_id=device,
            device_id_type=MESH,
        )

    def arrived(number):
        message(number, own, z_in.at[0], partner).wait_recv()

    lane = lax.broadcasted_iota(jnp.int32, (1, WIDTH), 1)
    starts = jnp.zeros((1, WIDTH), jnp.int32)
    ends = jnp.zeros((1, WIDTH), jnp.int32)
    for d in range(NDOCS):
        length = len_ref[d]
        starts = starts + jnp.where(lane > d, length, 0)
        ends = ends + jnp.where(lane >= d, length, 0)

    def in_doc(first):
        position = first + lax.broadcasted_iota(jnp.int32, (TOKENS, WIDTH), 0)
        return (position >= starts) & (position < ends)

    lanes = lax.broadcasted_iota(jnp.int32, (TOKENS, WIDTH), 1)

    def key_features(first):
        flag = jnp.where((lanes >= LSE_LANE) & (lanes < FEATURES), 1.0, 0.0)
        return jnp.where(in_doc(first), 1.0, flag).astype(bf16)

    here = block * BLOCK + index * TOKENS

    own[:, :WIDTH] = k_ref[...]
    own[:, WIDTH:] = v_ref[...]

    lse_pad[...] = jnp.zeros_like(lse_pad)
    for i, piece in enumerate(three_parts(lse_ref[...] * (-1.0 / SCALE))):
        lse_pad[LSE_LANE + i * HEADS : LSE_LANE + (i + 1) * HEADS, :TOKENS] = piece
    by_token = lse_pad[...].T[:TOKENS, :]
    by_token = jnp.where(lanes < NDOCS, jnp.where(in_doc(here), 0.0, -FAR), by_token)
    head = lax.broadcasted_iota(jnp.int32, (HEADS, WIDTH), 0)
    head_lane = lax.broadcasted_iota(jnp.int32, (HEADS, WIDTH), 1)
    chosen = jnp.where((head_lane < NDOCS) | (lax.rem(head_lane, HEADS) == head), 1.0, 0.0)
    qx[:, :WIDTH] = q_ref[...]
    qx[:, WIDTH:] = (by_token[:, None, :] * chosen[None]).reshape(ROWS, WIDTH).astype(bf16)

    douts = do_ref[...]
    delta = jnp.sum(douts.astype(f32) * o_ref[...].astype(f32), axis=1, keepdims=True)
    high, middle, low = three_parts(-delta)
    row_lane = lax.broadcasted_iota(jnp.int32, (ROWS, WIDTH), 1)
    dox[:, :WIDTH] = douts
    dox[:, WIDTH:] = jnp.where(
        row_lane == 0, high, jnp.where(row_lane == 1, middle, jnp.where(row_lane == 2, low, 0.0))
    ).astype(bf16)
    q_t[...] = q_ref[...].T
    do_t[...] = douts.T
    key_lane = lax.broadcasted_iota(jnp.int32, (KEYS, WIDTH), 1)
    vx[:, WIDTH:] = jnp.where(key_lane < 3, 1.0, 0.0).astype(bf16)

    def half(i, keys, values, mask):
        rows = pl.ds(i * HALF, HALF)
        probs = jnp.exp2(dot(qx[rows, :], keys, 1, 1) * RATE)
        if mask is not None:
            probs = jnp.where(mask, probs, 0.0)
        dscores = (probs * dot(dox[rows, :], values, 1, 1)).astype(bf16)
        probs = probs.astype(bf16)
        dq = dot(dscores, keys[:, :WIDTH], 1, 0)
        dk = dot(q_t[:, rows], dscores, 1, 0)
        dv = dot(do_t[:, rows], probs, 1, 0)
        return dq, dk, dv

    own_keys = jnp.concatenate([k_ref[...], key_features(here)], axis=1)
    own_values = jnp.concatenate([v_ref[...], vx[:TOKENS, WIDTH:]], axis=1)
    dk_sum, dv_sum = 0.0, 0.0
    for i in range(2):
        token = lax.broadcasted_iota(jnp.int32, (HALF, TOKENS), 0) // HEADS + i * (HALF // HEADS)
        mask = lax.broadcasted_iota(jnp.int32, (HALF, TOKENS), 1) <= token
        dq, dk, dv = half(i, own_keys, own_values, mask)
        dq_acc[i * HALF : (i + 1) * HALF, :] = dq
        dk_sum, dv_sum = dk_sum + dk, dv_sum + dv
    diag[:, :WIDTH] = dk_sum.T
    diag[:, WIDTH:] = dv_sum.T

    pl.semaphore_wait(barrier, len(others))

    message(Z_IN, own, slots.at[slot_of(0, 0, 0)], behind(1)).start()
    message(Z_IN + 1, own, slots.at[slot_of(0, 1, 0)], behind(2)).start()

    def along_x(d, old, source):
        r = CHIPS - d
        message(
            X_IN + (r - 1) * 2 + old, source, slots.at[slot_of(r, old, 0)], column(d)
        ).start()

    def across(dx, old, source):
        message(C_IN + dx * 2 + old, source, slots.at[slot_of(dx, old, 1)], partner).start()

    for d in (1, 3, 2):
        @pl.when(x + d < CHIPS)
        def _():
            along_x(d, 1, own)

    @pl.when(core == 0)
    def _():
        across(0, 1, own)

    arrived(Z_IN)
    for d in (1, 3, 2):
        along_x(d, 0, slots.at[slot_of(0, 0, 0)])
    across(0, 0, slots.at[slot_of(0, 0, 0)])
    arrived(Z_IN + 1)
    for d in (1, 3, 2):
        @pl.when(x + d >= CHIPS)
        def _():
            along_x(d, 1, slots.at[slot_of(0, 1, 0)])

    @pl.when(core == 1)
    def _():
        across(0, 1, slots.at[slot_of(0, 1, 0)])

    def pass_on(dx, old):
        arrived(X_IN + (dx - 1) * 2 + old)
        across(dx, old, slots.at[slot_of(dx, old, 0)])

    def first_of(dx, old, other):
        from_x = lax.rem(x + dx, CHIPS)
        from_core = (1 - core) if other else core
        from_index = from_x * 2 + from_core
        if old == 0:
            back = 1
        else:
            back = jnp.where(from_index < index, 0, 2)
        return lax.rem(block - back + BLOCKS, BLOCKS) * BLOCK + from_index * TOKENS

    def assemble(pairs):
        for i, (dx, old) in enumerate(pairs):
            arrived(C_IN + dx * 2 + old)
            for other in range(2):
                rows = slice((i * 2 + other) * TOKENS, (i * 2 + other + 1) * TOKENS)
                slot = slot_of(dx, old, other)
                kx[rows, :WIDTH] = slots[slot, :, :WIDTH]
                kx[rows, WIDTH:] = key_features(first_of(dx, old, other))
                vx[rows, :WIDTH] = slots[slot, :, WIDTH:]

    def compute(i):
        dq, dk, dv = half(i, kx[...], vx[...], None)
        dq_acc[i * HALF : (i + 1) * HALF, :] += dq
        if i == 0:
            dk_acc[...] = dk
            dv_acc[...] = dv
        else:
            dk_acc[...] += dk
            dv_acc[...] += dv

    def give(pairs):
        dk = dk_acc[...].T.astype(bf16)
        dv = dv_acc[...].T.astype(bf16)
        for i, (dx, old) in enumerate(pairs):
            for other in range(2):
                rows = slice((i * 2 + other) * TOKENS, (i * 2 + other + 1) * TOKENS)
                part[slot_of(dx, old, other), :, :WIDTH] = dk[rows]
                part[slot_of(dx, old, other), :, WIDTH:] = dv[rows]
            message(
                C_OUT + dx * 2 + old, part.at[slot_of(dx, old, 1)], c_in.at[dx * 2 + old], partner
            ).start()

    def combine(dx, old):
        arrived(C_OUT + dx * 2 + old)
        place = (dx - 1) * 2 + old
        total = part[slot_of(dx, old, 0)].astype(f32) + c_in[dx * 2 + old].astype(f32)
        x_out[place] = total.astype(bf16)
        r = CHIPS - dx
        number = (r - 1) * 2 + old
        message(X_OUT + number, x_out.at[place], x_in.at[number], column(dx)).start()

    def taken(flag, value):
        return jnp.where(flag, value.astype(f32), 0.0)

    order = [
        [(1, 0), (3, 0)],
        [(1, 1), (3, 1)],
        [(0, 1), (2, 1)],
        [(0, 0), (2, 0)],
    ]
    pass_on(1, 0)
    pass_on(3, 0)
    assemble(order[0])
    compute(0)
    pass_on(1, 1)
    pass_on(3, 1)
    pass_on(2, 0)
    compute(1)
    give(order[0])
    pass_on(2, 1)
    assemble(order[1])
    compute(0)
    combine(1, 0)
    combine(3, 0)
    compute(1)
    give(order[1])
    assemble(order[2])
    compute(0)
    combine(1, 1)
    combine(3, 1)
    compute(1)
    give(order[2])
    assemble(order[3])
    compute(0)
    combine(2, 1)
    compute(1)
    give(order[3])

    for d in (1, 2, 3):
        arrived(X_OUT + (d - 1) * 2 + 1)
    arrived(C_OUT + 1)
    later = part[slot_of(0, 1, 0)].astype(f32) + taken(core == 1, c_in[1])
    for d in (1, 2, 3):
        later = later + taken(x + d >= CHIPS, x_in[(d - 1) * 2 + 1])
    z_out[1] = later.astype(bf16)
    message(Z_OUT + 1, z_out.at[1], z_in.at[1], behind(-2)).start()
    combine(2, 0)
    mine = diag[...] + taken(core == 0, c_in[1])
    for d in (1, 2, 3):
        mine = mine + taken(x + d < CHIPS, x_in[(d - 1) * 2 + 1])
    diag[...] = mine
    dq_ref[...] = (dq_acc[...] * SCALE).astype(bf16)
    arrived(C_OUT)
    total = part[slot_of(0, 0, 0)].astype(f32) + c_in[0].astype(f32)
    for d in (1, 3, 2):
        arrived(X_OUT + (d - 1) * 2)
        total = total + x_in[(d - 1) * 2].astype(f32)
    z_out[0] = total.astype(bf16)
    message(Z_OUT, z_out.at[0], z_in.at[0], behind(-1)).start()
    arrived(Z_OUT + 1)
    arrived(Z_OUT)
    mine = diag[...] + z_in[0].astype(f32) + z_in[1].astype(f32)
    dk_ref[...] = (mine[:, :WIDTH] * SCALE).astype(bf16)
    dv_ref[...] = mine[:, WIDTH:].astype(bf16)
    for number in range(MESSAGES):
        message(number, own, z_in.at[0], partner).wait_send()


def per_device(query, key, value, output, grad_out, lse, doc_lengths):
    vmem = pl.BlockSpec(memory_space=pltpu.VMEM)
    chunk = (TOKENS, 2 * WIDTH)
    dq, dk, dv = pl.pallas_call(
        kernel,
        out_shape=(
            jax.ShapeDtypeStruct((ROWS, WIDTH), bf16),
            jax.ShapeDtypeStruct((TOKENS, WIDTH), bf16),
            jax.ShapeDtypeStruct((TOKENS, WIDTH), bf16),
        ),
        in_specs=[pl.BlockSpec(memory_space=pltpu.SMEM)] + [vmem] * 6,
        out_specs=(vmem, vmem, vmem),
        scratch_shapes=[
            pltpu.VMEM(chunk, bf16),
            pltpu.VMEM((16,) + chunk, bf16),
            pltpu.VMEM((ROWS, 2 * WIDTH), bf16),
            pltpu.VMEM((ROWS, 2 * WIDTH), bf16),
            pltpu.VMEM((WIDTH, ROWS), bf16),
            pltpu.VMEM((WIDTH, ROWS), bf16),
            pltpu.VMEM((KEYS, 2 * WIDTH), bf16),
            pltpu.VMEM((KEYS, 2 * WIDTH), bf16),
            pltpu.VMEM((ROWS, WIDTH), f32),
            pltpu.VMEM((WIDTH, KEYS), f32),
            pltpu.VMEM((WIDTH, KEYS), f32),
            pltpu.VMEM((WIDTH, 2 * WIDTH), f32),
            pltpu.VMEM(chunk, f32),
            pltpu.VMEM((16,) + chunk, bf16),
            pltpu.VMEM((8,) + chunk, bf16),
            pltpu.VMEM((6,) + chunk, bf16),
            pltpu.VMEM((6,) + chunk, bf16),
            pltpu.VMEM((2,) + chunk, bf16),
            pltpu.VMEM((2,) + chunk, bf16),
            pltpu.SemaphoreType.DMA((MESSAGES,)),
            pltpu.SemaphoreType.DMA((MESSAGES,)),
        ],
        compiler_params=pltpu.CompilerParams(
            collective_id=0, has_side_effects=True, vmem_limit_bytes=56 * 2**20
        ),
    )(
        doc_lengths,
        query.reshape(ROWS, WIDTH),
        key,
        value,
        output.reshape(ROWS, WIDTH),
        grad_out.reshape(ROWS, WIDTH),
        lse,
    )
    return (dq.reshape(TOKENS, HEADS, WIDTH), dk, dv)


def solution(mesh):
    tokens = P(("blk", "ulysses"), None, None)
    rows = P(("blk", "ulysses"), None)
    return jax.shard_map(
        per_device,
        mesh=mesh,
        in_specs=(tokens, rows, rows, tokens, tokens, P(None, ("blk", "ulysses")), P()),
        out_specs=(tokens, rows, rows),
        check_vma=False,
    )
```

```python
import math

import jax
import jax.numpy as jnp
from jax import lax
from jax.experimental import pallas as pl
from jax.experimental.pallas import tpu as pltpu
from jax.sharding import PartitionSpec as P

f32 = jnp.float32
bf16 = jnp.bfloat16
MESH = pl.DeviceIdType.MESH

HEADS = 8
WIDTH = 128
TOKENS = 192
ROWS = TOKENS * HEADS
GROUPS = 8
BLOCK = TOKENS * GROUPS
BLOCKS = 32
CHIPS = 4
NDOCS = 32
KEYS = 4 * TOKENS
HALF = ROWS // 2
SCALE = WIDTH ** -0.5
RATE = SCALE * math.log2(math.e)
FAR = float(2 ** 17)
LSE_LANE = NDOCS
FEATURES = NDOCS + 3 * HEADS

Z_IN = 0
X_IN = 2
C_IN = 8
C_OUT = 16
X_OUT = 24
Z_OUT = 30
MESSAGES = 32


def dot(a, b, ca, cb):
    return lax.dot_general(a, b, (((ca,), (cb,)), ((), ())), preferred_element_type=f32)


def three_parts(value):
    high = value.astype(bf16).astype(f32)
    middle = (value - high).astype(bf16).astype(f32)
    return high, middle, value - high - middle


def slot_of(dx, old, other):
    return dx * 4 + old * 2 + other


def kernel(
    len_ref, q_ref, k_ref, v_ref, o_ref, do_ref, lse_ref,
    dq_ref, dk_ref, dv_ref,
    own, slots, qx, dox, q_t, do_t, outs, lse_in, kx, vx, dq_acc, dk_acc, dv_acc, lse_pad,
    diag, part, c_in, x_out, x_in, z_out, z_in, result, send_sem, recv_sem, load_sem, store_sem,
):
    block = lax.axis_index("blk")
    index = lax.axis_index("ulysses")
    x = index // 2
    core = lax.rem(index, 2)

    def column(d):
        return {"blk": block, "ulysses": lax.rem(x + d, CHIPS) * 2 + core}

    def behind(steps):
        return {"blk": lax.rem(block + steps + BLOCKS, BLOCKS), "ulysses": index}

    partner = {"blk": block, "ulysses": x * 2 + 1 - core}

    def exists(steps):
        return (block + steps >= 0) & (block + steps < BLOCKS)

    barrier = pltpu.get_barrier_semaphore()
    for device in [partner] + [column(d) for d in (1, 2, 3)]:
        pl.semaphore_signal(barrier, inc=1, device_id=device, device_id_type=MESH)
    greeted = 4
    for steps in (2, -2, 1, -1):
        @pl.when(exists(steps))
        def _():
            pl.semaphore_signal(barrier, inc=1, device_id=behind(steps), device_id_type=MESH)
        greeted = greeted + jnp.where(exists(steps), 1, 0)

    loads = [
        pltpu.make_async_copy(source, target, load_sem.at[i])
        for i, (source, target) in enumerate([
            (k_ref, own.at[:, :WIDTH]),
            (v_ref, own.at[:, WIDTH:]),
            (lse_ref, lse_in),
            (do_ref, dox.at[:, :WIDTH]),
            (o_ref, outs),
            (q_ref, qx.at[:, :WIDTH]),
        ])
    ]
    for load in loads:
        load.start()

    def message(number, source, target, device):
        return pltpu.make_async_remote_copy(
            src_ref=source,
            dst_ref=target,
            send_sem=send_sem.at[number],
            recv_sem=recv_sem.at[number],
            device_id=device,
            device_id_type=MESH,
        )

    def arrived(number):
        message(number, own, z_in.at[0], partner).wait_recv()

    def along_x(d, old, source):
        r = CHIPS - d
        message(
            X_IN + (r - 1) * 2 + old, source, slots.at[slot_of(r, old, 0)], column(d)
        ).start()

    def across(dx, old, source):
        message(C_IN + dx * 2 + old, source, slots.at[slot_of(dx, old, 1)], partner).start()

    loads[0].wait()
    loads[1].wait()
    pl.semaphore_wait(barrier, greeted)
    for steps in (1, 2):
        @pl.when(exists(steps))
        def _():
            target = slots.at[slot_of(0, steps - 1, 0)]
            message(Z_IN + steps - 1, own, target, behind(steps)).start()

        @pl.when(~exists(-steps))
        def _():
            slots[slot_of(0, steps - 1, 0)] = jnp.zeros((TOKENS, 2 * WIDTH), bf16)

    for d in (1, 3, 2):
        @pl.when(x + d < CHIPS)
        def _():
            along_x(d, 1, own)

    @pl.when(core == 0)
    def _():
        across(0, 1, own)

    lane = lax.broadcasted_iota(jnp.int32, (1, WIDTH), 1)
    starts = jnp.zeros((1, WIDTH), jnp.int32)
    ends = jnp.zeros((1, WIDTH), jnp.int32)
    for d in range(NDOCS):
        length = len_ref[d]
        starts = starts + jnp.where(lane > d, length, 0)
        ends = ends + jnp.where(lane >= d, length, 0)

    def in_doc(first):
        position = first + lax.broadcasted_iota(jnp.int32, (TOKENS, WIDTH), 0)
        return (position >= starts) & (position < ends)

    lanes = lax.broadcasted_iota(jnp.int32, (TOKENS, WIDTH), 1)

    def key_features(first):
        flag = jnp.where((lanes >= LSE_LANE) & (lanes < FEATURES), 1.0, 0.0)
        return jnp.where(in_doc(first), 1.0, flag).astype(bf16)

    here = block * BLOCK + index * TOKENS

    loads[2].wait()
    lse_pad[...] = jnp.zeros_like(lse_pad)
    for i, piece in enumerate(three_parts(lse_in[...] * (-1.0 / SCALE))):
        lse_pad[LSE_LANE + i * HEADS : LSE_LANE + (i + 1) * HEADS, :TOKENS] = piece
    by_token = lse_pad[...].T[:TOKENS, :]
    by_token = jnp.where(lanes < NDOCS, jnp.where(in_doc(here), 0.0, -FAR), by_token)
    head = lax.broadcasted_iota(jnp.int32, (HEADS, WIDTH), 0)
    head_lane = lax.broadcasted_iota(jnp.int32, (HEADS, WIDTH), 1)
    chosen = jnp.where((head_lane < NDOCS) | (lax.rem(head_lane, HEADS) == head), 1.0, 0.0)
    qx[:, WIDTH:] = (by_token[:, None, :] * chosen[None]).reshape(ROWS, WIDTH).astype(bf16)

    loads[3].wait()
    loads[4].wait()
    douts = dox[:, :WIDTH]
    delta = jnp.sum(douts.astype(f32) * outs[...].astype(f32), axis=1, keepdims=True)
    high, middle, low = three_parts(-delta)
    row_lane = lax.broadcasted_iota(jnp.int32, (ROWS, WIDTH), 1)
    dox[:, WIDTH:] = jnp.where(
        row_lane == 0, high, jnp.where(row_lane == 1, middle, jnp.where(row_lane == 2, low, 0.0))
    ).astype(bf16)
    do_t[...] = douts.T
    loads[5].wait()
    q_t[...] = qx[:, :WIDTH].T
    key_lane = lax.broadcasted_iota(jnp.int32, (KEYS, WIDTH), 1)
    vx[:, WIDTH:] = jnp.where(key_lane < 3, 1.0, 0.0).astype(bf16)

    def half(i, keys, values, mask):
        rows = pl.ds(i * HALF, HALF)
        probs = jnp.exp2(dot(qx[rows, :], keys, 1, 1) * RATE)
        if mask is not None:
            probs = jnp.where(mask, probs, 0.0)
        dscores = (probs * dot(dox[rows, :], values, 1, 1)).astype(bf16)
        probs = probs.astype(bf16)
        dq = dot(dscores, keys[:, :WIDTH], 1, 0)
        dk = dot(q_t[:, rows], dscores, 1, 0)
        dv = dot(do_t[:, rows], probs, 1, 0)
        return dq, dk, dv

    @pl.when(exists(-1))
    def _():
        arrived(Z_IN)

    for d in (1, 3, 2):
        along_x(d, 0, slots.at[slot_of(0, 0, 0)])
    across(0, 0, slots.at[slot_of(0, 0, 0)])

    own_keys = jnp.concatenate([own[:, :WIDTH], key_features(here)], axis=1)
    own_values = jnp.concatenate([own[:, WIDTH:], vx[:TOKENS, WIDTH:]], axis=1)
    dk_sum, dv_sum = 0.0, 0.0
    for i in range(2):
        token = lax.broadcasted_iota(jnp.int32, (HALF, TOKENS), 0) // HEADS + i * (HALF // HEADS)
        mask = lax.broadcasted_iota(jnp.int32, (HALF, TOKENS), 1) <= token
        dq, dk, dv = half(i, own_keys, own_values, mask)
        dq_acc[i * HALF : (i + 1) * HALF, :] = dq
        dk_sum, dv_sum = dk_sum + dk, dv_sum + dv
    diag[:, :WIDTH] = dk_sum.T
    diag[:, WIDTH:] = dv_sum.T

    def pass_on(dx, old):
        arrived(X_IN + (dx - 1) * 2 + old)
        across(dx, old, slots.at[slot_of(dx, old, 0)])

    def first_of(dx, old, other):
        from_x = lax.rem(x + dx, CHIPS)
        from_core = (1 - core) if other else core
        from_index = from_x * 2 + from_core
        if old == 0:
            back = 1
        else:
            back = jnp.where(from_index < index, 0, 2)
        return lax.rem(block - back + BLOCKS, BLOCKS) * BLOCK + from_index * TOKENS

    def assemble(pairs):
        for i, (dx, old) in enumerate(pairs):
            arrived(C_IN + dx * 2 + old)
            for other in range(2):
                rows = slice((i * 2 + other) * TOKENS, (i * 2 + other + 1) * TOKENS)
                slot = slot_of(dx, old, other)
                kx[rows, :WIDTH] = slots[slot, :, :WIDTH]
                kx[rows, WIDTH:] = key_features(first_of(dx, old, other))
                vx[rows, :WIDTH] = slots[slot, :, WIDTH:]

    def compute(pairs, i):
        keys = len(pairs) * 2 * TOKENS
        dq, dk, dv = half(i, kx[:keys, :], vx[:keys, :], None)
        dq_acc[i * HALF : (i + 1) * HALF, :] += dq
        if i == 0:
            dk_acc[:, :keys] = dk
            dv_acc[:, :keys] = dv
        else:
            dk_acc[:, :keys] += dk
            dv_acc[:, :keys] += dv

    def give(pairs):
        keys = len(pairs) * 2 * TOKENS
        dk = dk_acc[:, :keys].T.astype(bf16)
        dv = dv_acc[:, :keys].T.astype(bf16)
        for i, (dx, old) in enumerate(pairs):
            for other in range(2):
                rows = slice((i * 2 + other) * TOKENS, (i * 2 + other + 1) * TOKENS)
                part[slot_of(dx, old, other), :, :WIDTH] = dk[rows]
                part[slot_of(dx, old, other), :, WIDTH:] = dv[rows]
            message(
                C_OUT + dx * 2 + old, part.at[slot_of(dx, old, 1)], c_in.at[dx * 2 + old], partner
            ).start()

    def combine(dx, old):
        arrived(C_OUT + dx * 2 + old)
        place = (dx - 1) * 2 + old
        total = part[slot_of(dx, old, 0)].astype(f32) + c_in[dx * 2 + old].astype(f32)
        x_out[place] = total.astype(bf16)
        r = CHIPS - dx
        number = (r - 1) * 2 + old
        message(X_OUT + number, x_out.at[place], x_in.at[number], column(dx)).start()

    def taken(flag, value):
        return jnp.where(flag, value.astype(f32), 0.0)

    first = [(0, 0)]
    assemble(first)
    compute(first, 0)
    compute(first, 1)
    give(first)

    @pl.when(exists(-2))
    def _():
        arrived(Z_IN + 1)

    for d in (1, 3, 2):
        @pl.when(x + d >= CHIPS)
        def _():
            along_x(d, 1, slots.at[slot_of(0, 1, 0)])

    @pl.when(core == 1)
    def _():
        across(0, 1, slots.at[slot_of(0, 1, 0)])

    pass_on(1, 0)
    pass_on(3, 0)
    group = [(1, 0), (3, 0)]
    assemble(group)
    compute(group, 0)
    pass_on(2, 0)
    compute(group, 1)
    give(group)
    pass_on(1, 1)
    pass_on(3, 1)
    group = [(2, 0), (0, 1)]
    assemble(group)
    compute(group, 0)
    pass_on(2, 1)
    combine(1, 0)
    combine(3, 0)
    compute(group, 1)
    give(group)
    group = [(1, 1), (3, 1)]
    assemble(group)
    compute(group, 0)
    combine(2, 0)
    compute(group, 1)
    give(group)
    group = [(2, 1)]
    assemble(group)
    compute(group, 0)
    combine(1, 1)
    combine(3, 1)
    compute(group, 1)
    give(group)
    combine(2, 1)

    result[...] = (dq_acc[...] * SCALE).astype(bf16)
    store = pltpu.make_async_copy(result, dq_ref, store_sem.at[0])
    store.start()
    arrived(C_OUT)
    total = part[slot_of(0, 0, 0)].astype(f32) + c_in[0].astype(f32)
    for d in (1, 3, 2):
        arrived(X_OUT + (d - 1) * 2)
        total = total + x_in[(d - 1) * 2].astype(f32)
    z_out[0] = total.astype(bf16)

    @pl.when(exists(-1))
    def _():
        message(Z_OUT, z_out.at[0], z_in.at[0], behind(-1)).start()

    arrived(C_OUT + 1)
    later = part[slot_of(0, 1, 0)].astype(f32) + taken(core == 1, c_in[1])
    mine = diag[...] + taken(core == 0, c_in[1])
    for d in (1, 3, 2):
        arrived(X_OUT + (d - 1) * 2 + 1)
        later = later + taken(x + d >= CHIPS, x_in[(d - 1) * 2 + 1])
        mine = mine + taken(x + d < CHIPS, x_in[(d - 1) * 2 + 1])
    z_out[1] = later.astype(bf16)

    @pl.when(exists(-2))
    def _():
        message(Z_OUT + 1, z_out.at[1], z_in.at[1], behind(-2)).start()

    diag[...] = mine
    for steps in (1, 2):
        @pl.when(exists(steps))
        def _():
            arrived(Z_OUT + steps - 1)
            diag[...] += z_in[steps - 1].astype(f32)

    outs[:TOKENS, :] = (diag[:, :WIDTH] * SCALE).astype(bf16)
    outs[TOKENS : 2 * TOKENS, :] = diag[:, WIDTH:].astype(bf16)
    last = [
        pltpu.make_async_copy(outs.at[:TOKENS], dk_ref, store_sem.at[1]),
        pltpu.make_async_copy(outs.at[TOKENS : 2 * TOKENS], dv_ref, store_sem.at[2]),
    ]
    for copy in last:
        copy.start()
    for copy in [store] + last:
        copy.wait()
    for number in range(X_IN, Z_OUT):
        message(number, own, z_in.at[0], partner).wait_send()
    for steps in (1, 2):
        @pl.when(exists(steps))
        def _():
            message(Z_IN + steps - 1, own, z_in.at[0], partner).wait_send()

        @pl.when(exists(-steps))
        def _():
            message(Z_OUT + steps - 1, own, z_in.at[0], partner).wait_send()


def hand_over(dq_in, dk_in, dv_in, dq_out, dk_out, dv_out, sem):
    copies = [
        pltpu.make_async_copy(source, target, sem.at[i])
        for i, (source, target) in enumerate(
            [(dq_in, dq_out), (dk_in, dk_out), (dv_in, dv_out)]
        )
    ]
    for copy in copies:
        copy.start()
    for copy in copies:
        copy.wait()


def per_device(query, key, value, output, grad_out, lse, doc_lengths):
    anywhere = pl.BlockSpec(memory_space=pl.ANY)
    chunk = (TOKENS, 2 * WIDTH)
    shapes = (
        jax.ShapeDtypeStruct((ROWS, WIDTH), bf16),
        jax.ShapeDtypeStruct((TOKENS, WIDTH), bf16),
        jax.ShapeDtypeStruct((TOKENS, WIDTH), bf16),
    )
    grads = pl.pallas_call(
        kernel,
        out_shape=shapes,
        in_specs=[pl.BlockSpec(memory_space=pltpu.SMEM)] + [anywhere] * 6,
        out_specs=(anywhere,) * 3,
        scratch_shapes=[
            pltpu.VMEM(chunk, bf16),
            pltpu.VMEM((16,) + chunk, bf16),
            pltpu.VMEM((ROWS, 2 * WIDTH), bf16),
            pltpu.VMEM((ROWS, 2 * WIDTH), bf16),
            pltpu.VMEM((WIDTH, ROWS), bf16),
            pltpu.VMEM((WIDTH, ROWS), bf16),
            pltpu.VMEM((ROWS, WIDTH), bf16),
            pltpu.VMEM((HEADS, TOKENS), f32),
            pltpu.VMEM((KEYS, 2 * WIDTH), bf16),
            pltpu.VMEM((KEYS, 2 * WIDTH), bf16),
            pltpu.VMEM((ROWS, WIDTH), f32),
            pltpu.VMEM((WIDTH, KEYS), f32),
            pltpu.VMEM((WIDTH, KEYS), f32),
            pltpu.VMEM((WIDTH, 2 * WIDTH), f32),
            pltpu.VMEM(chunk, f32),
            pltpu.VMEM((16,) + chunk, bf16),
            pltpu.VMEM((8,) + chunk, bf16),
            pltpu.VMEM((6,) + chunk, bf16),
            pltpu.VMEM((6,) + chunk, bf16),
            pltpu.VMEM((2,) + chunk, bf16),
            pltpu.VMEM((2,) + chunk, bf16),
            pltpu.VMEM((ROWS, WIDTH), bf16),
            pltpu.SemaphoreType.DMA((MESSAGES,)),
            pltpu.SemaphoreType.DMA((MESSAGES,)),
            pltpu.SemaphoreType.DMA((6,)),
            pltpu.SemaphoreType.DMA((3,)),
        ],
        compiler_params=pltpu.CompilerParams(
            collective_id=0, has_side_effects=True, vmem_limit_bytes=56 * 2**20
        ),
    )(
        doc_lengths,
        query.reshape(ROWS, WIDTH),
        key,
        value,
        output.reshape(ROWS, WIDTH),
        grad_out.reshape(ROWS, WIDTH),
        lse,
    )
    dq, dk, dv = pl.pallas_call(
        hand_over,
        out_shape=shapes,
        in_specs=[anywhere] * 3,
        out_specs=(anywhere,) * 3,
        scratch_shapes=[pltpu.SemaphoreType.DMA((3,))],
    )(*grads)
    return (dq.reshape(TOKENS, HEADS, WIDTH), dk, dv)


def solution(mesh):
    tokens = P(("blk", "ulysses"), None, None)
    rows = P(("blk", "ulysses"), None)
    return jax.shard_map(
        per_device,
        mesh=mesh,
        in_specs=(tokens, rows, rows, tokens, tokens, P(None, ("blk", "ulysses")), P()),
        out_specs=(tokens, rows, rows),
        check_vma=False,
    )
```

```python
import math

import jax
import jax.numpy as jnp
from jax import lax
from jax.experimental import pallas as pl
from jax.experimental.pallas import tpu as pltpu
from jax.sharding import PartitionSpec as P

f32 = jnp.float32
bf16 = jnp.bfloat16
MESH = pl.DeviceIdType.MESH

HEADS = 8
WIDTH = 128
TOKENS = 192
ROWS = TOKENS * HEADS
GROUPS = 8
BLOCK = TOKENS * GROUPS
BLOCKS = 32
CHIPS = 4
NDOCS = 32
KEYS = 4 * TOKENS
HALF = ROWS // 2
SCALE = WIDTH ** -0.5
RATE = SCALE * math.log2(math.e)
FAR = float(2 ** 17)
LSE_LANE = NDOCS
FEATURES = NDOCS + 3 * HEADS

Z_IN = 0
X_IN = 2
C_IN = 8
C_OUT = 16
X_OUT = 24
Z_OUT = 30
MESSAGES = 32
PIECES = 2
PIECE = TOKENS // PIECES


def dot(a, b, ca, cb):
    return lax.dot_general(a, b, (((ca,), (cb,)), ((), ())), preferred_element_type=f32)


def three_parts(value):
    high = value.astype(bf16).astype(f32)
    middle = (value - high).astype(bf16).astype(f32)
    return high, middle, value - high - middle


def slot_of(dx, old, other):
    return dx * 4 + old * 2 + other


def kernel(
    len_ref, q_ref, k_ref, v_ref, o_ref, do_ref, lse_ref,
    dq_ref, dk_ref, dv_ref,
    own, slots, qx, dox, q_t, do_t, outs, lse_in, kx, vx, dq_acc, dk_acc, dv_acc, lse_pad,
    diag, part, c_in, x_out, x_in, z_out, z_in, result, send_sem, recv_sem, load_sem, store_sem,
):
    block = lax.axis_index("blk")
    index = lax.axis_index("ulysses")
    x = index // 2
    core = lax.rem(index, 2)

    def column(d):
        return {"blk": block, "ulysses": lax.rem(x + d, CHIPS) * 2 + core}

    def behind(steps):
        return {"blk": lax.rem(block + steps + BLOCKS, BLOCKS), "ulysses": index}

    partner = {"blk": block, "ulysses": x * 2 + 1 - core}

    def exists(steps):
        return (block + steps >= 0) & (block + steps < BLOCKS)

    barrier = pltpu.get_barrier_semaphore()
    for device in [partner] + [column(d) for d in (1, 2, 3)]:
        pl.semaphore_signal(barrier, inc=1, device_id=device, device_id_type=MESH)
    greeted = 4
    for steps in (2, -2, 1, -1):
        @pl.when(exists(steps))
        def _():
            pl.semaphore_signal(barrier, inc=1, device_id=behind(steps), device_id_type=MESH)
        greeted = greeted + jnp.where(exists(steps), 1, 0)

    loads = [
        pltpu.make_async_copy(source, target, load_sem.at[i])
        for i, (source, target) in enumerate([
            (k_ref, own.at[:, :WIDTH]),
            (v_ref, own.at[:, WIDTH:]),
            (lse_ref, lse_in),
            (do_ref, dox.at[:, :WIDTH]),
            (o_ref, outs),
            (q_ref, qx.at[:, :WIDTH]),
        ])
    ]
    for load in loads:
        load.start()

    def message(number, p, source, target, device):
        rows = pl.ds(p * PIECE, PIECE)
        return pltpu.make_async_remote_copy(
            src_ref=source.at[rows],
            dst_ref=target.at[rows],
            send_sem=send_sem.at[number * PIECES + p],
            recv_sem=recv_sem.at[number * PIECES + p],
            device_id=device,
            device_id_type=MESH,
        )

    def arrived(number, p):
        message(number, p, own, z_in.at[0], partner).wait_recv()

    def along_x(d, old, p, source):
        r = CHIPS - d
        message(
            X_IN + (r - 1) * 2 + old, p, source, slots.at[slot_of(r, old, 0)], column(d)
        ).start()

    def across(dx, old, p, source):
        message(C_IN + dx * 2 + old, p, source, slots.at[slot_of(dx, old, 1)], partner).start()

    loads[0].wait()
    loads[1].wait()
    pl.semaphore_wait(barrier, greeted)
    @pl.when(exists(1))
    def _():
        for p in range(PIECES):
            message(Z_IN, p, own, slots.at[slot_of(0, 0, 0)], behind(1)).start()

    for steps in (1, 2):
        @pl.when(~exists(-steps))
        def _():
            slots[slot_of(0, steps - 1, 0)] = jnp.zeros((TOKENS, 2 * WIDTH), bf16)

    for d in (1, 3, 2):
        @pl.when(x + d < CHIPS)
        def _():
            for p in range(PIECES):
                along_x(d, 1, p, own)

    @pl.when(core == 0)
    def _():
        for p in range(PIECES):
            across(0, 1, p, own)

    lane = lax.broadcasted_iota(jnp.int32, (1, WIDTH), 1)
    starts = jnp.zeros((1, WIDTH), jnp.int32)
    ends = jnp.zeros((1, WIDTH), jnp.int32)
    for d in range(NDOCS):
        length = len_ref[d]
        starts = starts + jnp.where(lane > d, length, 0)
        ends = ends + jnp.where(lane >= d, length, 0)

    def in_doc(first):
        position = first + lax.broadcasted_iota(jnp.int32, (TOKENS, WIDTH), 0)
        return (position >= starts) & (position < ends)

    lanes = lax.broadcasted_iota(jnp.int32, (TOKENS, WIDTH), 1)

    def key_features(first):
        flag = jnp.where((lanes >= LSE_LANE) & (lanes < FEATURES), 1.0, 0.0)
        return jnp.where(in_doc(first), 1.0, flag).astype(bf16)

    here = block * BLOCK + index * TOKENS

    loads[2].wait()
    lse_pad[...] = jnp.zeros_like(lse_pad)
    for i, piece in enumerate(three_parts(lse_in[...] * (-1.0 / SCALE))):
        lse_pad[LSE_LANE + i * HEADS : LSE_LANE + (i + 1) * HEADS, :TOKENS] = piece
    by_token = lse_pad[...].T[:TOKENS, :]
    by_token = jnp.where(lanes < NDOCS, jnp.where(in_doc(here), 0.0, -FAR), by_token)
    head = lax.broadcasted_iota(jnp.int32, (HEADS, WIDTH), 0)
    head_lane = lax.broadcasted_iota(jnp.int32, (HEADS, WIDTH), 1)
    chosen = jnp.where((head_lane < NDOCS) | (lax.rem(head_lane, HEADS) == head), 1.0, 0.0)
    qx[:, WIDTH:] = (by_token[:, None, :] * chosen[None]).reshape(ROWS, WIDTH).astype(bf16)

    loads[3].wait()
    loads[4].wait()
    douts = dox[:, :WIDTH]
    delta = jnp.sum(douts.astype(f32) * outs[...].astype(f32), axis=1, keepdims=True)
    high, middle, low = three_parts(-delta)
    row_lane = lax.broadcasted_iota(jnp.int32, (ROWS, WIDTH), 1)
    dox[:, WIDTH:] = jnp.where(
        row_lane == 0, high, jnp.where(row_lane == 1, middle, jnp.where(row_lane == 2, low, 0.0))
    ).astype(bf16)
    do_t[...] = douts.T
    loads[5].wait()
    q_t[...] = qx[:, :WIDTH].T
    key_lane = lax.broadcasted_iota(jnp.int32, (KEYS, WIDTH), 1)
    vx[:, WIDTH:] = jnp.where(key_lane < 3, 1.0, 0.0).astype(bf16)

    def half(i, keys, values, mask):
        rows = pl.ds(i * HALF, HALF)
        probs = jnp.exp2(dot(qx[rows, :], keys, 1, 1) * RATE)
        if mask is not None:
            probs = jnp.where(mask, probs, 0.0)
        dscores = (probs * dot(dox[rows, :], values, 1, 1)).astype(bf16)
        probs = probs.astype(bf16)
        dq = dot(dscores, keys[:, :WIDTH], 1, 0)
        dk = dot(q_t[:, rows], dscores, 1, 0)
        dv = dot(do_t[:, rows], probs, 1, 0)
        return dq, dk, dv

    before = slots.at[slot_of(0, 0, 0)]
    for p in range(PIECES):
        @pl.when(exists(-1))
        def _():
            arrived(Z_IN, p)

            @pl.when(exists(1))
            def _():
                message(Z_IN + 1, p, before, slots.at[slot_of(0, 1, 0)], behind(1)).start()

        for d in (1, 3, 2):
            along_x(d, 0, p, before)
        across(0, 0, p, before)

    own_keys = jnp.concatenate([own[:, :WIDTH], key_features(here)], axis=1)
    own_values = jnp.concatenate([own[:, WIDTH:], vx[:TOKENS, WIDTH:]], axis=1)
    dk_sum, dv_sum = 0.0, 0.0
    for i in range(2):
        token = lax.broadcasted_iota(jnp.int32, (HALF, TOKENS), 0) // HEADS + i * (HALF // HEADS)
        mask = lax.broadcasted_iota(jnp.int32, (HALF, TOKENS), 1) <= token
        dq, dk, dv = half(i, own_keys, own_values, mask)
        dq_acc[i * HALF : (i + 1) * HALF, :] = dq
        dk_sum, dv_sum = dk_sum + dk, dv_sum + dv
    diag[:, :WIDTH] = dk_sum.T
    diag[:, WIDTH:] = dv_sum.T

    def pass_on(dx, old):
        for p in range(PIECES):
            arrived(X_IN + (dx - 1) * 2 + old, p)
            across(dx, old, p, slots.at[slot_of(dx, old, 0)])

    def first_of(dx, old, other):
        from_x = lax.rem(x + dx, CHIPS)
        from_core = (1 - core) if other else core
        from_index = from_x * 2 + from_core
        if old == 0:
            back = 1
        else:
            back = jnp.where(from_index < index, 0, 2)
        return lax.rem(block - back + BLOCKS, BLOCKS) * BLOCK + from_index * TOKENS

    def assemble(pairs):
        for i, (dx, old) in enumerate(pairs):
            for p in range(PIECES):
                arrived(C_IN + dx * 2 + old, p)
            for other in range(2):
                rows = slice((i * 2 + other) * TOKENS, (i * 2 + other + 1) * TOKENS)
                slot = slot_of(dx, old, other)
                kx[rows, :WIDTH] = slots[slot, :, :WIDTH]
                kx[rows, WIDTH:] = key_features(first_of(dx, old, other))
                vx[rows, :WIDTH] = slots[slot, :, WIDTH:]

    def compute(pairs, i):
        keys = len(pairs) * 2 * TOKENS
        dq, dk, dv = half(i, kx[:keys, :], vx[:keys, :], None)
        dq_acc[i * HALF : (i + 1) * HALF, :] += dq
        if i == 0:
            dk_acc[:, :keys] = dk
            dv_acc[:, :keys] = dv
        else:
            dk_acc[:, :keys] += dk
            dv_acc[:, :keys] += dv

    def give(pairs):
        keys = len(pairs) * 2 * TOKENS
        dk = dk_acc[:, :keys].T.astype(bf16)
        dv = dv_acc[:, :keys].T.astype(bf16)
        for i, (dx, old) in enumerate(pairs):
            for other in range(2):
                rows = slice((i * 2 + other) * TOKENS, (i * 2 + other + 1) * TOKENS)
                part[slot_of(dx, old, other), :, :WIDTH] = dk[rows]
                part[slot_of(dx, old, other), :, WIDTH:] = dv[rows]
            for p in range(PIECES):
                message(
                    C_OUT + dx * 2 + old, p, part.at[slot_of(dx, old, 1)], c_in.at[dx * 2 + old],
                    partner,
                ).start()

    def combine(dx, old):
        place = (dx - 1) * 2 + old
        number = (CHIPS - dx - 1) * 2 + old
        for p in range(PIECES):
            rows = slice(p * PIECE, (p + 1) * PIECE)
            arrived(C_OUT + dx * 2 + old, p)
            total = part[slot_of(dx, old, 0), rows].astype(f32) + c_in[dx * 2 + old, rows].astype(f32)
            x_out[place, rows] = total.astype(bf16)
            message(X_OUT + number, p, x_out.at[place], x_in.at[number], column(dx)).start()

    def taken(flag, value):
        return jnp.where(flag, value.astype(f32), 0.0)

    first = [(0, 0)]
    assemble(first)
    compute(first, 0)
    compute(first, 1)
    give(first)

    before_that = slots.at[slot_of(0, 1, 0)]
    for p in range(PIECES):
        @pl.when(exists(-2))
        def _():
            arrived(Z_IN + 1, p)

        for d in (1, 3, 2):
            @pl.when(x + d >= CHIPS)
            def _():
                along_x(d, 1, p, before_that)

        @pl.when(core == 1)
        def _():
            across(0, 1, p, before_that)

    pass_on(1, 0)
    pass_on(3, 0)
    group = [(1, 0), (3, 0)]
    assemble(group)
    compute(group, 0)
    pass_on(2, 0)
    compute(group, 1)
    give(group)
    pass_on(1, 1)
    pass_on(3, 1)
    group = [(1, 1), (3, 1)]
    assemble(group)
    compute(group, 0)
    pass_on(2, 1)
    combine(1, 0)
    combine(3, 0)
    compute(group, 1)
    give(group)
    group = [(2, 1), (0, 1)]
    assemble(group)
    compute(group, 0)
    combine(1, 1)
    combine(3, 1)
    compute(group, 1)
    give(group)
    group = [(2, 0)]
    assemble(group)
    compute(group, 0)
    combine(2, 1)
    compute(group, 1)
    give(group)
    combine(2, 0)

    result[...] = (dq_acc[...] * SCALE).astype(bf16)
    store = pltpu.make_async_copy(result, dq_ref, store_sem.at[0])
    store.start()
    for p in range(PIECES):
        rows = slice(p * PIECE, (p + 1) * PIECE)
        arrived(C_OUT + 1, p)
        later = part[slot_of(0, 1, 0), rows].astype(f32) + taken(core == 1, c_in[1, rows])
        mine = diag[rows] + taken(core == 0, c_in[1, rows])
        for d in (1, 3, 2):
            arrived(X_OUT + (d - 1) * 2 + 1, p)
            received = x_in[(d - 1) * 2 + 1, rows]
            later = later + taken(x + d >= CHIPS, received)
            mine = mine + taken(x + d < CHIPS, received)
        z_out[1, rows] = later.astype(bf16)
        diag[rows] = mine

        @pl.when(exists(-2))
        def _():
            message(Z_OUT + 1, p, z_out.at[1], z_in.at[1], behind(-2)).start()

    for p in range(PIECES):
        rows = slice(p * PIECE, (p + 1) * PIECE)
        arrived(C_OUT, p)
        total = part[slot_of(0, 0, 0), rows].astype(f32) + c_in[0, rows].astype(f32)
        for d in (1, 3, 2):
            arrived(X_OUT + (d - 1) * 2, p)
            total = total + x_in[(d - 1) * 2, rows].astype(f32)
        z_out[0, rows] = total.astype(bf16)

        @pl.when(exists(-1))
        def _():
            message(Z_OUT, p, z_out.at[0], z_in.at[0], behind(-1)).start()

    for steps in (2, 1):
        @pl.when(exists(steps))
        def _():
            for p in range(PIECES):
                rows = slice(p * PIECE, (p + 1) * PIECE)
                arrived(Z_OUT + steps - 1, p)
                diag[rows] += z_in[steps - 1, rows].astype(f32)

    outs[:TOKENS, :] = (diag[:, :WIDTH] * SCALE).astype(bf16)
    outs[TOKENS : 2 * TOKENS, :] = diag[:, WIDTH:].astype(bf16)
    last = [
        pltpu.make_async_copy(outs.at[:TOKENS], dk_ref, store_sem.at[1]),
        pltpu.make_async_copy(outs.at[TOKENS : 2 * TOKENS], dv_ref, store_sem.at[2]),
    ]
    for copy in last:
        copy.start()
    for copy in [store] + last:
        copy.wait()

    def left(number):
        for p in range(PIECES):
            message(number, p, own, z_in.at[0], partner).wait_send()

    for number in range(X_IN, Z_OUT):
        left(number)
    for steps in (1, 2):
        @pl.when(exists(1) & exists(1 - steps))
        def _():
            left(Z_IN + steps - 1)

        @pl.when(exists(-steps))
        def _():
            left(Z_OUT + steps - 1)


def hand_over(dq_in, dk_in, dv_in, dq_out, dk_out, dv_out):
    dq_out[...] = dq_in[...]
    dk_out[...] = dk_in[...]
    dv_out[...] = dv_in[...]


def per_device(query, key, value, output, grad_out, lse, doc_lengths):
    anywhere = pl.BlockSpec(memory_space=pl.ANY)
    chunk = (TOKENS, 2 * WIDTH)
    shapes = (
        jax.ShapeDtypeStruct((ROWS, WIDTH), bf16),
        jax.ShapeDtypeStruct((TOKENS, WIDTH), bf16),
        jax.ShapeDtypeStruct((TOKENS, WIDTH), bf16),
    )
    grads = pl.pallas_call(
        kernel,
        out_shape=shapes,
        in_specs=[pl.BlockSpec(memory_space=pltpu.SMEM)] + [anywhere] * 6,
        out_specs=(anywhere,) * 3,
        scratch_shapes=[
            pltpu.VMEM(chunk, bf16),
            pltpu.VMEM((16,) + chunk, bf16),
            pltpu.VMEM((ROWS, 2 * WIDTH), bf16),
            pltpu.VMEM((ROWS, 2 * WIDTH), bf16),
            pltpu.VMEM((WIDTH, ROWS), bf16),
            pltpu.VMEM((WIDTH, ROWS), bf16),
            pltpu.VMEM((ROWS, WIDTH), bf16),
            pltpu.VMEM((HEADS, TOKENS), f32),
            pltpu.VMEM((KEYS, 2 * WIDTH), bf16),
            pltpu.VMEM((KEYS, 2 * WIDTH), bf16),
            pltpu.VMEM((ROWS, WIDTH), f32),
            pltpu.VMEM((WIDTH, KEYS), f32),
            pltpu.VMEM((WIDTH, KEYS), f32),
            pltpu.VMEM((WIDTH, 2 * WIDTH), f32),
            pltpu.VMEM(chunk, f32),
            pltpu.VMEM((16,) + chunk, bf16),
            pltpu.VMEM((8,) + chunk, bf16),
            pltpu.VMEM((6,) + chunk, bf16),
            pltpu.VMEM((6,) + chunk, bf16),
            pltpu.VMEM((2,) + chunk, bf16),
            pltpu.VMEM((2,) + chunk, bf16),
            pltpu.VMEM((ROWS, WIDTH), bf16),
            pltpu.SemaphoreType.DMA((MESSAGES * PIECES,)),
            pltpu.SemaphoreType.DMA((MESSAGES * PIECES,)),
            pltpu.SemaphoreType.DMA((6,)),
            pltpu.SemaphoreType.DMA((3,)),
        ],
        compiler_params=pltpu.CompilerParams(
            collective_id=0, has_side_effects=True, vmem_limit_bytes=56 * 2**20
        ),
    )(
        doc_lengths,
        query.reshape(ROWS, WIDTH),
        key,
        value,
        output.reshape(ROWS, WIDTH),
        grad_out.reshape(ROWS, WIDTH),
        lse,
    )
    dq, dk, dv = pl.pallas_call(
        hand_over,
        out_shape=shapes,
        in_specs=[pl.BlockSpec(memory_space=pltpu.VMEM)] * 3,
        out_specs=(pl.BlockSpec(memory_space=pltpu.VMEM),) * 3,
    )(*grads)
    return (dq.reshape(TOKENS, HEADS, WIDTH), dk, dv)


def solution(mesh):
    tokens = P(("blk", "ulysses"), None, None)
    rows = P(("blk", "ulysses"), None)
    return jax.shard_map(
        per_device,
        mesh=mesh,
        in_specs=(tokens, rows, rows, tokens, tokens, P(None, ("blk", "ulysses")), P()),
        out_specs=(tokens, rows, rows),
        check_vma=False,
    )
```

```python
import math

import jax
import jax.numpy as jnp
from jax import lax
from jax.experimental import pallas as pl
from jax.experimental.pallas import tpu as pltpu
from jax.sharding import PartitionSpec as P

f32 = jnp.float32
bf16 = jnp.bfloat16
MESH = pl.DeviceIdType.MESH

HEADS = 8
WIDTH = 128
TOKENS = 192
ROWS = TOKENS * HEADS
GROUPS = 8
BLOCK = TOKENS * GROUPS
BLOCKS = 32
CHIPS = 4
NDOCS = 32
KEYS = 4 * TOKENS
HALF = ROWS // 2
SCALE = WIDTH ** -0.5
RATE = SCALE * math.log2(math.e)
FAR = float(2 ** 17)
LSE_LANE = NDOCS
FEATURES = NDOCS + 3 * HEADS

Z_IN = 0
X_IN = 2
C_IN = 8
C_OUT = 16
X_OUT = 24
Z_OUT = 30
MESSAGES = 32
PIECES = {Z_IN: 2, X_IN: 2, C_IN: 2, C_OUT: 2, X_OUT: 2, Z_OUT: 2}
MOST = 2


def pieces(number):
    return PIECES[max(first for first in PIECES if first <= number)]


def within(number, p, other):
    mine, its = pieces(number), pieces(other)
    if its >= mine:
        return range(p * its // mine, (p + 1) * its // mine)
    return range(p * its // mine, p * its // mine + 1) if p % (mine // its) == 0 else range(0)


def dot(a, b, ca, cb):
    return lax.dot_general(a, b, (((ca,), (cb,)), ((), ())), preferred_element_type=f32)


def three_parts(value):
    high = value.astype(bf16).astype(f32)
    middle = (value - high).astype(bf16).astype(f32)
    return high, middle, value - high - middle


def slot_of(dx, old, other):
    return dx * 4 + old * 2 + other


def kernel(
    len_ref, q_ref, k_ref, v_ref, o_ref, do_ref, lse_ref,
    dq_ref, dk_ref, dv_ref,
    own, slots, qx, dox, q_t, do_t, outs, lse_in, kx, vx, dq_acc, dk_acc, dv_acc, lse_pad,
    diag, total_acc, part, c_in, x_out, x_in, z_out, z_in, result, send_sem, recv_sem, load_sem, store_sem,
):
    block = lax.axis_index("blk")
    index = lax.axis_index("ulysses")
    x = index // 2
    core = lax.rem(index, 2)

    def column(d):
        return {"blk": block, "ulysses": lax.rem(x + d, CHIPS) * 2 + core}

    def behind(steps):
        return {"blk": lax.rem(block + steps + BLOCKS, BLOCKS), "ulysses": index}

    partner = {"blk": block, "ulysses": x * 2 + 1 - core}

    def exists(steps):
        return (block + steps >= 0) & (block + steps < BLOCKS)

    barrier = pltpu.get_barrier_semaphore()
    for device in [partner] + [column(d) for d in (1, 2, 3)]:
        pl.semaphore_signal(barrier, inc=1, device_id=device, device_id_type=MESH)
    greeted = 4
    for steps in (1, -1):
        @pl.when(exists(steps))
        def _():
            pl.semaphore_signal(barrier, inc=1, device_id=behind(steps), device_id_type=MESH)
        greeted = greeted + jnp.where(exists(steps), 1, 0)

    loads = [
        pltpu.make_async_copy(source, target, load_sem.at[i])
        for i, (source, target) in enumerate([
            (k_ref, own.at[:, :WIDTH]),
            (v_ref, own.at[:, WIDTH:]),
            (lse_ref, lse_in),
            (do_ref, dox.at[:, :WIDTH]),
            (o_ref, outs),
            (q_ref, qx.at[:, :WIDTH]),
        ])
    ]
    for load in loads:
        load.start()

    def message(number, p, source, target, device):
        size = TOKENS // pieces(number)
        rows = pl.ds(p * size, size)
        return pltpu.make_async_remote_copy(
            src_ref=source.at[rows],
            dst_ref=target.at[rows],
            send_sem=send_sem.at[number * MOST + p],
            recv_sem=recv_sem.at[number * MOST + p],
            device_id=device,
            device_id_type=MESH,
        )

    def arrived(number, p):
        message(number, p, own, z_in.at[0], partner).wait_recv()

    def along_x(d, old, p, source):
        r = CHIPS - d
        message(
            X_IN + (r - 1) * 2 + old, p, source, slots.at[slot_of(r, old, 0)], column(d)
        ).start()

    def across(dx, old, p, source):
        message(C_IN + dx * 2 + old, p, source, slots.at[slot_of(dx, old, 1)], partner).start()

    loads[0].wait()
    loads[1].wait()
    pl.semaphore_wait(barrier, greeted)
    @pl.when(exists(1))
    def _():
        for p in range(pieces(Z_IN)):
            message(Z_IN, p, own, slots.at[slot_of(0, 0, 0)], behind(1)).start()

    for steps in (1, 2):
        @pl.when(~exists(-steps))
        def _():
            slots[slot_of(0, steps - 1, 0)] = jnp.zeros((TOKENS, 2 * WIDTH), bf16)

    for d in (1, 3, 2):
        @pl.when(x + d < CHIPS)
        def _():
            for p in range(pieces(X_IN)):
                along_x(d, 1, p, own)

    @pl.when(core == 0)
    def _():
        for p in range(pieces(C_IN)):
            across(0, 1, p, own)

    lane = lax.broadcasted_iota(jnp.int32, (1, WIDTH), 1)
    starts = jnp.zeros((1, WIDTH), jnp.int32)
    ends = jnp.zeros((1, WIDTH), jnp.int32)
    for d in range(NDOCS):
        length = len_ref[d]
        starts = starts + jnp.where(lane > d, length, 0)
        ends = ends + jnp.where(lane >= d, length, 0)

    def in_doc(first):
        position = first + lax.broadcasted_iota(jnp.int32, (TOKENS, WIDTH), 0)
        return (position >= starts) & (position < ends)

    lanes = lax.broadcasted_iota(jnp.int32, (TOKENS, WIDTH), 1)

    def key_features(first):
        flag = jnp.where((lanes >= LSE_LANE) & (lanes < FEATURES), 1.0, 0.0)
        return jnp.where(in_doc(first), 1.0, flag).astype(bf16)

    here = block * BLOCK + index * TOKENS

    loads[2].wait()
    lse_pad[...] = jnp.zeros_like(lse_pad)
    for i, piece in enumerate(three_parts(lse_in[...] * (-1.0 / SCALE))):
        lse_pad[LSE_LANE + i * HEADS : LSE_LANE + (i + 1) * HEADS, :TOKENS] = piece
    by_token = lse_pad[...].T[:TOKENS, :]
    by_token = jnp.where(lanes < NDOCS, jnp.where(in_doc(here), 0.0, -FAR), by_token)
    head = lax.broadcasted_iota(jnp.int32, (HEADS, WIDTH), 0)
    head_lane = lax.broadcasted_iota(jnp.int32, (HEADS, WIDTH), 1)
    chosen = jnp.where((head_lane < NDOCS) | (lax.rem(head_lane, HEADS) == head), 1.0, 0.0)
    qx[:, WIDTH:] = (by_token[:, None, :] * chosen[None]).reshape(ROWS, WIDTH).astype(bf16)

    loads[3].wait()
    loads[4].wait()
    douts = dox[:, :WIDTH]
    delta = jnp.sum(douts.astype(f32) * outs[...].astype(f32), axis=1, keepdims=True)
    high, middle, low = three_parts(-delta)
    row_lane = lax.broadcasted_iota(jnp.int32, (ROWS, WIDTH), 1)
    dox[:, WIDTH:] = jnp.where(
        row_lane == 0, high, jnp.where(row_lane == 1, middle, jnp.where(row_lane == 2, low, 0.0))
    ).astype(bf16)
    do_t[...] = douts.T
    loads[5].wait()
    q_t[...] = qx[:, :WIDTH].T
    key_lane = lax.broadcasted_iota(jnp.int32, (KEYS, WIDTH), 1)
    vx[:, WIDTH:] = jnp.where(key_lane < 3, 1.0, 0.0).astype(bf16)

    def half(i, keys, values, mask):
        rows = pl.ds(i * HALF, HALF)
        probs = jnp.exp2(dot(qx[rows, :], keys, 1, 1) * RATE)
        if mask is not None:
            probs = jnp.where(mask, probs, 0.0)
        dscores = (probs * dot(dox[rows, :], values, 1, 1)).astype(bf16)
        probs = probs.astype(bf16)
        dq = dot(dscores, keys[:, :WIDTH], 1, 0)
        dk = dot(q_t[:, rows], dscores, 1, 0)
        dv = dot(do_t[:, rows], probs, 1, 0)
        return dq, dk, dv

    before = slots.at[slot_of(0, 0, 0)]
    for p in range(pieces(X_IN)):
        @pl.when(exists(-1))
        def _():
            for q in within(X_IN, p, Z_IN):
                arrived(Z_IN, q)

                @pl.when(exists(1))
                def _():
                    message(Z_IN + 1, q, before, slots.at[slot_of(0, 1, 0)], behind(1)).start()

        for d in (1, 3, 2):
            along_x(d, 0, p, before)
    for p in range(pieces(C_IN)):
        across(0, 0, p, before)

    own_keys = jnp.concatenate([own[:, :WIDTH], key_features(here)], axis=1)
    own_values = jnp.concatenate([own[:, WIDTH:], vx[:TOKENS, WIDTH:]], axis=1)
    dk_sum, dv_sum = 0.0, 0.0
    for i in range(2):
        token = lax.broadcasted_iota(jnp.int32, (HALF, TOKENS), 0) // HEADS + i * (HALF // HEADS)
        mask = lax.broadcasted_iota(jnp.int32, (HALF, TOKENS), 1) <= token
        dq, dk, dv = half(i, own_keys, own_values, mask)
        dq_acc[i * HALF : (i + 1) * HALF, :] = dq
        dk_sum, dv_sum = dk_sum + dk, dv_sum + dv
    diag[:, :WIDTH] = dk_sum.T
    diag[:, WIDTH:] = dv_sum.T

    def pass_on(dx, old):
        came, goes = X_IN + (dx - 1) * 2 + old, C_IN + dx * 2 + old
        for p in range(pieces(goes)):
            for q in within(goes, p, came):
                arrived(came, q)
            across(dx, old, p, slots.at[slot_of(dx, old, 0)])

    def first_of(dx, old, other):
        from_x = lax.rem(x + dx, CHIPS)
        from_core = (1 - core) if other else core
        from_index = from_x * 2 + from_core
        if old == 0:
            back = 1
        else:
            back = jnp.where(from_index < index, 0, 2)
        return lax.rem(block - back + BLOCKS, BLOCKS) * BLOCK + from_index * TOKENS

    def assemble(pairs):
        for i, (dx, old) in enumerate(pairs):
            for p in range(pieces(C_IN)):
                arrived(C_IN + dx * 2 + old, p)
            for other in range(2):
                rows = slice((i * 2 + other) * TOKENS, (i * 2 + other + 1) * TOKENS)
                slot = slot_of(dx, old, other)
                kx[rows, :WIDTH] = slots[slot, :, :WIDTH]
                kx[rows, WIDTH:] = key_features(first_of(dx, old, other))
                vx[rows, :WIDTH] = slots[slot, :, WIDTH:]

    def compute(pairs, i):
        keys = len(pairs) * 2 * TOKENS
        dq, dk, dv = half(i, kx[:keys, :], vx[:keys, :], None)
        dq_acc[i * HALF : (i + 1) * HALF, :] += dq
        if i == 0:
            dk_acc[:, :keys] = dk
            dv_acc[:, :keys] = dv
        else:
            dk_acc[:, :keys] += dk
            dv_acc[:, :keys] += dv

    def give(pairs):
        keys = len(pairs) * 2 * TOKENS
        dk = dk_acc[:, :keys].astype(bf16).T
        dv = dv_acc[:, :keys].astype(bf16).T
        for i, (dx, old) in enumerate(pairs):
            for other in range(2):
                rows = slice((i * 2 + other) * TOKENS, (i * 2 + other + 1) * TOKENS)
                part[slot_of(dx, old, other), :, :WIDTH] = dk[rows]
                part[slot_of(dx, old, other), :, WIDTH:] = dv[rows]
            for p in range(pieces(C_OUT)):
                message(
                    C_OUT + dx * 2 + old, p, part.at[slot_of(dx, old, 1)], c_in.at[dx * 2 + old],
                    partner,
                ).start()

    def combine(dx, old):
        place = (dx - 1) * 2 + old
        number = (CHIPS - dx - 1) * 2 + old
        for p in range(pieces(X_OUT)):
            size = TOKENS // pieces(X_OUT)
            rows = slice(p * size, (p + 1) * size)
            for q in within(X_OUT, p, C_OUT):
                arrived(C_OUT + dx * 2 + old, q)
            total = part[slot_of(dx, old, 0), rows].astype(f32) + c_in[dx * 2 + old, rows].astype(f32)
            x_out[place, rows] = total.astype(bf16)
            message(X_OUT + number, p, x_out.at[place], x_in.at[number], column(dx)).start()

    def taken(flag, value):
        return jnp.where(flag, value.astype(f32), 0.0)

    group = [(0, 0)]
    assemble(group)
    compute(group, 0)
    compute(group, 1)
    give(group)
    before_that = slots.at[slot_of(0, 1, 0)]
    for p in range(pieces(X_IN)):
        @pl.when(exists(-2))
        def _():
            for q in within(X_IN, p, Z_IN + 1):
                arrived(Z_IN + 1, q)

        for d in (2, 1, 3):
            @pl.when(x + d >= CHIPS)
            def _():
                along_x(d, 1, p, before_that)

    @pl.when(core == 1)
    def _():
        for p in range(pieces(C_IN)):
            across(0, 1, p, before_that)

    pass_on(1, 0)
    pass_on(3, 0)
    group = [(1, 0), (3, 0)]
    assemble(group)
    compute(group, 0)
    pass_on(2, 0)
    compute(group, 1)
    give(group)
    pass_on(1, 1)
    pass_on(2, 1)
    group = [(1, 1), (2, 1)]
    assemble(group)
    compute(group, 0)
    pass_on(3, 1)
    combine(1, 0)
    combine(3, 0)
    compute(group, 1)
    give(group)
    group = [(3, 1), (0, 1)]
    assemble(group)
    compute(group, 0)
    combine(2, 1)
    combine(1, 1)
    compute(group, 1)
    give(group)
    group = [(2, 0)]
    assemble(group)
    compute(group, 0)
    combine(3, 1)
    compute(group, 1)
    give(group)
    combine(2, 0)

    result[...] = (dq_acc[...] * SCALE).astype(bf16)
    store = pltpu.make_async_copy(result, dq_ref, store_sem.at[0])
    store.start()
    size = TOKENS // pieces(Z_OUT)
    for p in range(pieces(Z_OUT)):
        rows = slice(p * size, (p + 1) * size)
        for q in within(Z_OUT, p, C_OUT):
            arrived(C_OUT + 1, q)
        later = part[slot_of(0, 1, 0), rows].astype(f32) + taken(core == 1, c_in[1, rows])
        mine = diag[rows] + taken(core == 0, c_in[1, rows])
        for d in (1, 3, 2):
            for q in within(Z_OUT, p, X_OUT):
                arrived(X_OUT + (d - 1) * 2 + 1, q)
            received = x_in[(d - 1) * 2 + 1, rows]
            later = later + taken(x + d >= CHIPS, received)
            mine = mine + taken(x + d < CHIPS, received)
        z_out[1, rows] = later.astype(bf16)
        diag[rows] = mine

        @pl.when(exists(-2))
        def _():
            message(Z_OUT + 1, p, z_out.at[1], z_in.at[1], behind(-1)).start()

    for p in range(pieces(Z_OUT)):
        rows = slice(p * size, (p + 1) * size)
        for q in within(Z_OUT, p, C_OUT):
            arrived(C_OUT, q)
        total = part[slot_of(0, 0, 0), rows].astype(f32) + c_in[0, rows].astype(f32)
        for d in (1, 3, 2):
            for q in within(Z_OUT, p, X_OUT):
                arrived(X_OUT + (d - 1) * 2, q)
            total = total + x_in[(d - 1) * 2, rows].astype(f32)
        total_acc[rows] = total

        @pl.when(exists(1) & exists(-1))
        def _():
            arrived(Z_OUT + 1, p)
            total_acc[rows] += z_in[1, rows].astype(f32)

        z_out[0, rows] = total_acc[rows].astype(bf16)

        @pl.when(exists(-1))
        def _():
            message(Z_OUT, p, z_out.at[0], z_in.at[0], behind(-1)).start()

    def left(number):
        for p in range(pieces(number)):
            message(number, p, own, z_in.at[0], partner).wait_send()

    for number in range(X_IN, Z_OUT):
        left(number)
    for steps in (1, 2):
        @pl.when(exists(1) & exists(1 - steps))
        def _():
            left(Z_IN + steps - 1)

    @pl.when(exists(1))
    def _():
        for p in range(pieces(Z_OUT)):
            rows = slice(p * size, (p + 1) * size)
            arrived(Z_OUT, p)
            diag[rows] += z_in[0, rows].astype(f32)

    outs[:TOKENS, :] = (diag[:, :WIDTH] * SCALE).astype(bf16)
    outs[TOKENS : 2 * TOKENS, :] = diag[:, WIDTH:].astype(bf16)
    last = [
        pltpu.make_async_copy(outs.at[:TOKENS], dk_ref, store_sem.at[1]),
        pltpu.make_async_copy(outs.at[TOKENS : 2 * TOKENS], dv_ref, store_sem.at[2]),
    ]
    for copy in last:
        copy.start()
    for steps in (1, 2):
        @pl.when(exists(-steps))
        def _():
            left(Z_OUT + steps - 1)

    for copy in [store] + last:
        copy.wait()


def hand_over(dq_in, dk_in, dv_in, dq_out, dk_out, dv_out):
    dq_out[...] = dq_in[...]
    dk_out[...] = dk_in[...]
    dv_out[...] = dv_in[...]


def per_device(query, key, value, output, grad_out, lse, doc_lengths):
    anywhere = pl.BlockSpec(memory_space=pl.ANY)
    chunk = (TOKENS, 2 * WIDTH)
    shapes = (
        jax.ShapeDtypeStruct((ROWS, WIDTH), bf16),
        jax.ShapeDtypeStruct((TOKENS, WIDTH), bf16),
        jax.ShapeDtypeStruct((TOKENS, WIDTH), bf16),
    )
    grads = pl.pallas_call(
        kernel,
        out_shape=shapes,
        in_specs=[pl.BlockSpec(memory_space=pltpu.SMEM)] + [anywhere] * 6,
        out_specs=(anywhere,) * 3,
        scratch_shapes=[
            pltpu.VMEM(chunk, bf16),
            pltpu.VMEM((16,) + chunk, bf16),
            pltpu.VMEM((ROWS, 2 * WIDTH), bf16),
            pltpu.VMEM((ROWS, 2 * WIDTH), bf16),
            pltpu.VMEM((WIDTH, ROWS), bf16),
            pltpu.VMEM((WIDTH, ROWS), bf16),
            pltpu.VMEM((ROWS, WIDTH), bf16),
            pltpu.VMEM((HEADS, TOKENS), f32),
            pltpu.VMEM((KEYS, 2 * WIDTH), bf16),
            pltpu.VMEM((KEYS, 2 * WIDTH), bf16),
            pltpu.VMEM((ROWS, WIDTH), f32),
            pltpu.VMEM((WIDTH, KEYS), f32),
            pltpu.VMEM((WIDTH, KEYS), f32),
            pltpu.VMEM((WIDTH, 2 * WIDTH), f32),
            pltpu.VMEM(chunk, f32),
            pltpu.VMEM(chunk, f32),
            pltpu.VMEM((16,) + chunk, bf16),
            pltpu.VMEM((8,) + chunk, bf16),
            pltpu.VMEM((6,) + chunk, bf16),
            pltpu.VMEM((6,) + chunk, bf16),
            pltpu.VMEM((2,) + chunk, bf16),
            pltpu.VMEM((2,) + chunk, bf16),
            pltpu.VMEM((ROWS, WIDTH), bf16),
            pltpu.SemaphoreType.DMA((MESSAGES * MOST,)),
            pltpu.SemaphoreType.DMA((MESSAGES * MOST,)),
            pltpu.SemaphoreType.DMA((6,)),
            pltpu.SemaphoreType.DMA((3,)),
        ],
        compiler_params=pltpu.CompilerParams(
            collective_id=0, has_side_effects=True, vmem_limit_bytes=56 * 2**20
        ),
    )(
        doc_lengths,
        query.reshape(ROWS, WIDTH),
        key,
        value,
        output.reshape(ROWS, WIDTH),
        grad_out.reshape(ROWS, WIDTH),
        lse,
    )
    dq, dk, dv = pl.pallas_call(
        hand_over,
        out_shape=shapes,
        in_specs=[pl.BlockSpec(memory_space=pltpu.VMEM)] * 3,
        out_specs=(pl.BlockSpec(memory_space=pltpu.VMEM),) * 3,
    )(*grads)
    return (dq.reshape(TOKENS, HEADS, WIDTH), dk, dv)


def solution(mesh):
    tokens = P(("blk", "ulysses"), None, None)
    rows = P(("blk", "ulysses"), None)
    return jax.shard_map(
        per_device,
        mesh=mesh,
        in_specs=(tokens, rows, rows, tokens, tokens, P(None, ("blk", "ulysses")), P()),
        out_specs=(tokens, rows, rows),
        check_vma=False,
    )
```

```python
import math

import jax
import jax.numpy as jnp
from jax import lax
from jax.experimental import pallas as pl
from jax.experimental.pallas import tpu as pltpu
from jax.sharding import PartitionSpec as P

f32 = jnp.float32
bf16 = jnp.bfloat16
MESH = pl.DeviceIdType.MESH

HEADS = 8
WIDTH = 128
TOKENS = 192
ROWS = TOKENS * HEADS
GROUPS = 8
BLOCK = TOKENS * GROUPS
BLOCKS = 32
CHIPS = 4
NDOCS = 32
KEYS = 4 * TOKENS
HALF = ROWS // 2
SCALE = WIDTH ** -0.5
RATE = SCALE * math.log2(math.e)
FAR = float(2 ** 17)
LSE_LANE = NDOCS
FEATURES = NDOCS + 3 * HEADS

Z_IN = 0
X_IN = 2
C_IN = 8
C_OUT = 16
X_OUT = 24
Z_OUT = 30
MESSAGES = 32
PIECES = {Z_IN: 2, X_IN: 2, C_IN: 2, C_OUT: 2, X_OUT: 2, Z_OUT: 2}
MOST = 2


def pieces(number):
    return PIECES[max(first for first in PIECES if first <= number)]


def within(number, p, other):
    mine, its = pieces(number), pieces(other)
    if its >= mine:
        return range(p * its // mine, (p + 1) * its // mine)
    return range(p * its // mine, p * its // mine + 1) if p % (mine // its) == 0 else range(0)


def dot(a, b, ca, cb):
    return lax.dot_general(a, b, (((ca,), (cb,)), ((), ())), preferred_element_type=f32)


def three_parts(value):
    high = value.astype(bf16).astype(f32)
    middle = (value - high).astype(bf16).astype(f32)
    return high, middle, value - high - middle


def slot_of(dx, old, other):
    return dx * 4 + old * 2 + other


def kernel(
    len_ref, q_ref, k_ref, v_ref, o_ref, do_ref, lse_ref,
    dq_ref, dk_ref, dv_ref,
    own, slots, qx, dox, q_t, do_t, outs, lse_in, kx, vx, dq_acc, dk_acc, dv_acc, lse_pad,
    diag, total_acc, part, c_in, x_out, x_in, z_out, z_in, result, send_sem, recv_sem, load_sem, store_sem,
):
    block = lax.axis_index("blk")
    index = lax.axis_index("ulysses")
    x = index // 2
    core = lax.rem(index, 2)

    def column(d):
        return {"blk": block, "ulysses": lax.rem(x + d, CHIPS) * 2 + core}

    def behind(steps):
        return {"blk": lax.rem(block + steps + BLOCKS, BLOCKS), "ulysses": index}

    partner = {"blk": block, "ulysses": x * 2 + 1 - core}

    def exists(steps):
        return (block + steps >= 0) & (block + steps < BLOCKS)

    barrier = pltpu.get_barrier_semaphore()
    for device in [partner] + [column(d) for d in (1, 2, 3)]:
        pl.semaphore_signal(barrier, inc=1, device_id=device, device_id_type=MESH)
    greeted = 4
    for steps in (1, -1):
        @pl.when(exists(steps))
        def _():
            pl.semaphore_signal(barrier, inc=1, device_id=behind(steps), device_id_type=MESH)
        greeted = greeted + jnp.where(exists(steps), 1, 0)

    loads = [
        pltpu.make_async_copy(source, target, load_sem.at[i])
        for i, (source, target) in enumerate([
            (k_ref, own.at[:, :WIDTH]),
            (v_ref, own.at[:, WIDTH:]),
            (lse_ref, lse_in),
            (do_ref, dox.at[:, :WIDTH]),
            (o_ref, outs),
            (q_ref, qx.at[:, :WIDTH]),
        ])
    ]
    for load in loads:
        load.start()

    def message(number, p, source, target, device):
        size = TOKENS // pieces(number)
        rows = pl.ds(p * size, size)
        return pltpu.make_async_remote_copy(
            src_ref=source.at[rows],
            dst_ref=target.at[rows],
            send_sem=send_sem.at[number * MOST + p],
            recv_sem=recv_sem.at[number * MOST + p],
            device_id=device,
            device_id_type=MESH,
        )

    def arrived(number, p):
        message(number, p, own, z_in.at[0], partner).wait_recv()

    def along_x(d, old, p, source):
        r = CHIPS - d
        message(
            X_IN + (r - 1) * 2 + old, p, source, slots.at[slot_of(r, old, 0)], column(d)
        ).start()

    def across(dx, old, p, source):
        message(C_IN + dx * 2 + old, p, source, slots.at[slot_of(dx, old, 1)], partner).start()

    loads[0].wait()
    loads[1].wait()
    pl.semaphore_wait(barrier, greeted)
    @pl.when(exists(1))
    def _():
        for p in range(pieces(Z_IN)):
            message(Z_IN, p, own, slots.at[slot_of(0, 0, 0)], behind(1)).start()

    for steps in (1, 2):
        @pl.when(~exists(-steps))
        def _():
            slots[slot_of(0, steps - 1, 0)] = jnp.zeros((TOKENS, 2 * WIDTH), bf16)

    for d in (1, 3, 2):
        @pl.when(x + d < CHIPS)
        def _():
            for p in range(pieces(X_IN)):
                along_x(d, 1, p, own)

    @pl.when(core == 0)
    def _():
        for p in range(pieces(C_IN)):
            across(0, 1, p, own)

    lane = lax.broadcasted_iota(jnp.int32, (1, WIDTH), 1)
    starts = jnp.zeros((1, WIDTH), jnp.int32)
    ends = jnp.zeros((1, WIDTH), jnp.int32)
    for d in range(NDOCS):
        length = len_ref[d]
        starts = starts + jnp.where(lane > d, length, 0)
        ends = ends + jnp.where(lane >= d, length, 0)

    def in_doc(first):
        position = first + lax.broadcasted_iota(jnp.int32, (TOKENS, WIDTH), 0)
        return (position >= starts) & (position < ends)

    lanes = lax.broadcasted_iota(jnp.int32, (TOKENS, WIDTH), 1)

    def key_features(first):
        flag = jnp.where((lanes >= LSE_LANE) & (lanes < FEATURES), 1.0, 0.0)
        return jnp.where(in_doc(first), 1.0, flag).astype(bf16)

    here = block * BLOCK + index * TOKENS

    loads[2].wait()
    lse_pad[...] = jnp.zeros_like(lse_pad)
    for i, piece in enumerate(three_parts(lse_in[...] * (-1.0 / SCALE))):
        lse_pad[LSE_LANE + i * HEADS : LSE_LANE + (i + 1) * HEADS, :TOKENS] = piece
    by_token = lse_pad[...].T[:TOKENS, :]
    by_token = jnp.where(lanes < NDOCS, jnp.where(in_doc(here), 0.0, -FAR), by_token)
    head = lax.broadcasted_iota(jnp.int32, (HEADS, WIDTH), 0)
    head_lane = lax.broadcasted_iota(jnp.int32, (HEADS, WIDTH), 1)
    chosen = jnp.where((head_lane < NDOCS) | (lax.rem(head_lane, HEADS) == head), 1.0, 0.0)
    qx[:, WIDTH:] = (by_token[:, None, :] * chosen[None]).reshape(ROWS, WIDTH).astype(bf16)

    loads[3].wait()
    loads[4].wait()
    douts = dox[:, :WIDTH]
    delta = jnp.sum(douts.astype(f32) * outs[...].astype(f32), axis=1, keepdims=True)
    high, middle, low = three_parts(-delta)
    row_lane = lax.broadcasted_iota(jnp.int32, (ROWS, WIDTH), 1)
    dox[:, WIDTH:] = jnp.where(
        row_lane == 0, high, jnp.where(row_lane == 1, middle, jnp.where(row_lane == 2, low, 0.0))
    ).astype(bf16)
    do_t[...] = douts.T
    loads[5].wait()
    q_t[...] = qx[:, :WIDTH].T
    key_lane = lax.broadcasted_iota(jnp.int32, (KEYS, WIDTH), 1)
    vx[:, WIDTH:] = jnp.where(key_lane < 3, 1.0, 0.0).astype(bf16)

    def half(i, keys, values, mask):
        rows = pl.ds(i * HALF, HALF)
        probs = jnp.exp2(dot(qx[rows, :], keys, 1, 1) * RATE)
        if mask is not None:
            probs = jnp.where(mask, probs, 0.0)
        dscores = (probs * dot(dox[rows, :], values, 1, 1)).astype(bf16)
        probs = probs.astype(bf16)
        dq = dot(dscores, keys[:, :WIDTH], 1, 0)
        dk = dot(q_t[:, rows], dscores, 1, 0)
        dv = dot(do_t[:, rows], probs, 1, 0)
        return dq, dk, dv

    before = slots.at[slot_of(0, 0, 0)]
    for p in range(pieces(X_IN)):
        @pl.when(exists(-1))
        def _():
            for q in within(X_IN, p, Z_IN):
                arrived(Z_IN, q)

                @pl.when(exists(1))
                def _():
                    message(Z_IN + 1, q, before, slots.at[slot_of(0, 1, 0)], behind(1)).start()

        for d in (1, 3, 2):
            along_x(d, 0, p, before)
        across(0, 0, p, before)

    own_keys = jnp.concatenate([own[:, :WIDTH], key_features(here)], axis=1)
    own_values = jnp.concatenate([own[:, WIDTH:], vx[:TOKENS, WIDTH:]], axis=1)
    dk_sum, dv_sum = 0.0, 0.0
    for i in range(2):
        token = lax.broadcasted_iota(jnp.int32, (HALF, TOKENS), 0) // HEADS + i * (HALF // HEADS)
        mask = lax.broadcasted_iota(jnp.int32, (HALF, TOKENS), 1) <= token
        dq, dk, dv = half(i, own_keys, own_values, mask)
        dq_acc[i * HALF : (i + 1) * HALF, :] = dq
        dk_sum, dv_sum = dk_sum + dk, dv_sum + dv
    diag[:, :WIDTH] = dk_sum.T
    diag[:, WIDTH:] = dv_sum.T

    def pass_on(dx, old):
        came, goes = X_IN + (dx - 1) * 2 + old, C_IN + dx * 2 + old
        for p in range(pieces(goes)):
            for q in within(goes, p, came):
                arrived(came, q)
            across(dx, old, p, slots.at[slot_of(dx, old, 0)])

    def first_of(dx, old, other):
        from_x = lax.rem(x + dx, CHIPS)
        from_core = (1 - core) if other else core
        from_index = from_x * 2 + from_core
        if old == 0:
            back = 1
        else:
            back = jnp.where(from_index < index, 0, 2)
        return lax.rem(block - back + BLOCKS, BLOCKS) * BLOCK + from_index * TOKENS

    def assemble(pairs):
        for i, (dx, old) in enumerate(pairs):
            for p in range(pieces(C_IN)):
                arrived(C_IN + dx * 2 + old, p)
            for other in range(2):
                rows = slice((i * 2 + other) * TOKENS, (i * 2 + other + 1) * TOKENS)
                slot = slot_of(dx, old, other)
                kx[rows, :WIDTH] = slots[slot, :, :WIDTH]
                kx[rows, WIDTH:] = key_features(first_of(dx, old, other))
                vx[rows, :WIDTH] = slots[slot, :, WIDTH:]

    def compute(pairs, i):
        keys = len(pairs) * 2 * TOKENS
        dq, dk, dv = half(i, kx[:keys, :], vx[:keys, :], None)
        dq_acc[i * HALF : (i + 1) * HALF, :] += dq
        if i == 0:
            dk_acc[:, :keys] = dk
            dv_acc[:, :keys] = dv
        else:
            dk_acc[:, :keys] += dk
            dv_acc[:, :keys] += dv

    def give(pairs):
        keys = len(pairs) * 2 * TOKENS
        dk = dk_acc[:, :keys].astype(bf16).T
        dv = dv_acc[:, :keys].astype(bf16).T
        for i, (dx, old) in enumerate(pairs):
            for other in range(2):
                rows = slice((i * 2 + other) * TOKENS, (i * 2 + other + 1) * TOKENS)
                part[slot_of(dx, old, other), :, :WIDTH] = dk[rows]
                part[slot_of(dx, old, other), :, WIDTH:] = dv[rows]
            for p in range(pieces(C_OUT)):
                message(
                    C_OUT + dx * 2 + old, p, part.at[slot_of(dx, old, 1)], c_in.at[dx * 2 + old],
                    partner,
                ).start()

    def combine(dx, old):
        place = (dx - 1) * 2 + old
        number = (CHIPS - dx - 1) * 2 + old
        for p in range(pieces(X_OUT)):
            size = TOKENS // pieces(X_OUT)
            rows = slice(p * size, (p + 1) * size)
            for q in within(X_OUT, p, C_OUT):
                arrived(C_OUT + dx * 2 + old, q)
            total = part[slot_of(dx, old, 0), rows].astype(f32) + c_in[dx * 2 + old, rows].astype(f32)
            x_out[place, rows] = total.astype(bf16)
            message(X_OUT + number, p, x_out.at[place], x_in.at[number], column(dx)).start()

    def taken(flag, value):
        return jnp.where(flag, value.astype(f32), 0.0)

    group = [(0, 0)]
    assemble(group)
    compute(group, 0)
    before_that = slots.at[slot_of(0, 1, 0)]
    for p in range(pieces(X_IN)):
        @pl.when(exists(-2))
        def _():
            for q in within(X_IN, p, Z_IN + 1):
                arrived(Z_IN + 1, q)

        for d in (2, 1, 3):
            @pl.when(x + d >= CHIPS)
            def _():
                along_x(d, 1, p, before_that)

    @pl.when(core == 1)
    def _():
        for p in range(pieces(C_IN)):
            across(0, 1, p, before_that)

    compute(group, 1)
    give(group)
    pass_on(1, 0)
    pass_on(3, 0)
    group = [(1, 0), (3, 0)]
    assemble(group)
    compute(group, 0)
    pass_on(2, 0)
    compute(group, 1)
    give(group)
    pass_on(1, 1)
    pass_on(2, 1)
    group = [(1, 1), (2, 1)]
    assemble(group)
    compute(group, 0)
    pass_on(3, 1)
    combine(1, 0)
    combine(3, 0)
    compute(group, 1)
    give(group)
    group = [(3, 1), (0, 1)]
    assemble(group)
    compute(group, 0)
    combine(2, 1)
    combine(1, 1)
    compute(group, 1)
    give(group)
    group = [(2, 0)]
    assemble(group)
    compute(group, 0)
    combine(3, 1)
    compute(group, 1)
    give(group)
    combine(2, 0)

    result[...] = (dq_acc[...] * SCALE).astype(bf16)
    store = pltpu.make_async_copy(result, dq_ref, store_sem.at[0])
    store.start()
    size = TOKENS // pieces(Z_OUT)
    for p in range(pieces(Z_OUT)):
        rows = slice(p * size, (p + 1) * size)
        for q in within(Z_OUT, p, C_OUT):
            arrived(C_OUT + 1, q)
        later = part[slot_of(0, 1, 0), rows].astype(f32) + taken(core == 1, c_in[1, rows])
        mine = diag[rows] + taken(core == 0, c_in[1, rows])
        for d in (1, 3, 2):
            for q in within(Z_OUT, p, X_OUT):
                arrived(X_OUT + (d - 1) * 2 + 1, q)
            received = x_in[(d - 1) * 2 + 1, rows]
            later = later + taken(x + d >= CHIPS, received)
            mine = mine + taken(x + d < CHIPS, received)
        z_out[1, rows] = later.astype(bf16)
        diag[rows] = mine

        @pl.when(exists(-2))
        def _():
            message(Z_OUT + 1, p, z_out.at[1], z_in.at[1], behind(-1)).start()

    for p in range(pieces(Z_OUT)):
        rows = slice(p * size, (p + 1) * size)
        for q in within(Z_OUT, p, C_OUT):
            arrived(C_OUT, q)
        total = part[slot_of(0, 0, 0), rows].astype(f32) + c_in[0, rows].astype(f32)
        for d in (1, 3, 2):
            for q in within(Z_OUT, p, X_OUT):
                arrived(X_OUT + (d - 1) * 2, q)
            total = total + x_in[(d - 1) * 2, rows].astype(f32)
        total_acc[rows] = total

        @pl.when(exists(1) & exists(-1))
        def _():
            arrived(Z_OUT + 1, p)
            total_acc[rows] += z_in[1, rows].astype(f32)

        z_out[0, rows] = total_acc[rows].astype(bf16)

        @pl.when(exists(-1))
        def _():
            message(Z_OUT, p, z_out.at[0], z_in.at[0], behind(-1)).start()

    def left(number):
        for p in range(pieces(number)):
            message(number, p, own, z_in.at[0], partner).wait_send()

    for number in range(X_IN, Z_OUT):
        left(number)
    for steps in (1, 2):
        @pl.when(exists(1) & exists(1 - steps))
        def _():
            left(Z_IN + steps - 1)

    @pl.when(exists(1))
    def _():
        for p in range(pieces(Z_OUT)):
            rows = slice(p * size, (p + 1) * size)
            arrived(Z_OUT, p)
            diag[rows] += z_in[0, rows].astype(f32)

    outs[:TOKENS, :] = (diag[:, :WIDTH] * SCALE).astype(bf16)
    outs[TOKENS : 2 * TOKENS, :] = diag[:, WIDTH:].astype(bf16)
    last = [
        pltpu.make_async_copy(outs.at[:TOKENS], dk_ref, store_sem.at[1]),
        pltpu.make_async_copy(outs.at[TOKENS : 2 * TOKENS], dv_ref, store_sem.at[2]),
    ]
    for copy in last:
        copy.start()
    for steps in (1, 2):
        @pl.when(exists(-steps))
        def _():
            left(Z_OUT + steps - 1)

    for copy in [store] + last:
        copy.wait()


def hand_over(dq_in, dk_in, dv_in, dq_out, dk_out, dv_out):
    dq_out[...] = dq_in[...]
    dk_out[...] = dk_in[...]
    dv_out[...] = dv_in[...]


def per_device(query, key, value, output, grad_out, lse, doc_lengths):
    anywhere = pl.BlockSpec(memory_space=pl.ANY)
    chunk = (TOKENS, 2 * WIDTH)
    shapes = (
        jax.ShapeDtypeStruct((ROWS, WIDTH), bf16),
        jax.ShapeDtypeStruct((TOKENS, WIDTH), bf16),
        jax.ShapeDtypeStruct((TOKENS, WIDTH), bf16),
    )
    grads = pl.pallas_call(
        kernel,
        out_shape=shapes,
        in_specs=[pl.BlockSpec(memory_space=pltpu.SMEM)] + [anywhere] * 6,
        out_specs=(anywhere,) * 3,
        scratch_shapes=[
            pltpu.VMEM(chunk, bf16),
            pltpu.VMEM((16,) + chunk, bf16),
            pltpu.VMEM((ROWS, 2 * WIDTH), bf16),
            pltpu.VMEM((ROWS, 2 * WIDTH), bf16),
            pltpu.VMEM((WIDTH, ROWS), bf16),
            pltpu.VMEM((WIDTH, ROWS), bf16),
            pltpu.VMEM((ROWS, WIDTH), bf16),
            pltpu.VMEM((HEADS, TOKENS), f32),
            pltpu.VMEM((KEYS, 2 * WIDTH), bf16),
            pltpu.VMEM((KEYS, 2 * WIDTH), bf16),
            pltpu.VMEM((ROWS, WIDTH), f32),
            pltpu.VMEM((WIDTH, KEYS), f32),
            pltpu.VMEM((WIDTH, KEYS), f32),
            pltpu.VMEM((WIDTH, 2 * WIDTH), f32),
            pltpu.VMEM(chunk, f32),
            pltpu.VMEM(chunk, f32),
            pltpu.VMEM((16,) + chunk, bf16),
            pltpu.VMEM((8,) + chunk, bf16),
            pltpu.VMEM((6,) + chunk, bf16),
            pltpu.VMEM((6,) + chunk, bf16),
            pltpu.VMEM((2,) + chunk, bf16),
            pltpu.VMEM((2,) + chunk, bf16),
            pltpu.VMEM((ROWS, WIDTH), bf16),
            pltpu.SemaphoreType.DMA((MESSAGES * MOST,)),
            pltpu.SemaphoreType.DMA((MESSAGES * MOST,)),
            pltpu.SemaphoreType.DMA((6,)),
            pltpu.SemaphoreType.DMA((3,)),
        ],
        compiler_params=pltpu.CompilerParams(
            collective_id=0, has_side_effects=True, vmem_limit_bytes=56 * 2**20
        ),
    )(
        doc_lengths,
        query.reshape(ROWS, WIDTH),
        key,
        value,
        output.reshape(ROWS, WIDTH),
        grad_out.reshape(ROWS, WIDTH),
        lse,
    )
    dq, dk, dv = pl.pallas_call(
        hand_over,
        out_shape=shapes,
        in_specs=[pl.BlockSpec(memory_space=pltpu.VMEM)] * 3,
        out_specs=(pl.BlockSpec(memory_space=pltpu.VMEM),) * 3,
    )(*grads)
    return (dq.reshape(TOKENS, HEADS, WIDTH), dk, dv)


def solution(mesh):
    tokens = P(("blk", "ulysses"), None, None)
    rows = P(("blk", "ulysses"), None)
    return jax.shard_map(
        per_device,
        mesh=mesh,
        in_specs=(tokens, rows, rows, tokens, tokens, P(None, ("blk", "ulysses")), P()),
        out_specs=(tokens, rows, rows),
        check_vma=False,
    )
```
